512 devices in a mesh: seq: 64 (over x, y_hi, z), tensor: 8 (over y_lo, core).
Axes of the slice: x: 4, y: 8 (y_hi: 2, y_lo: 4; y = y_hi * 4 + y_lo), z: 8, core: 2. Of those that a mesh axis runs over, the one named last changes fastest.
Arguments:
- queries: bfloat16 [16384, 8192], P('seq', 'tensor'), may hold values from -6 to 6
- features: bfloat16 [6144, 4096], P('seq'), may hold values from -6 to 6
- w_key: bfloat16 [4096, 1024], P(None, 'tensor'), may hold values from -0.09375 to 0.09375
- w_value: bfloat16 [4096, 1024], P(None, 'tensor'), may hold values from -0.5 to 0.5
- q_gain: float32 [128], replicated, may hold values from 0.1 to 1.9
- k_gain: float32 [128], replicated, may hold values from 0.1 to 1.9
- slot_image: int32 [64], replicated, may hold values from 0 to 63, as said below
- image_tiles: int32 [64], replicated, may hold values from 1 to 4
- image_range: int32 [256, 2], P('seq'), may hold values from 0 to 64, as said below
- d_out: bfloat16 [16384, 8192], P('seq', 'tensor'), may hold values from -6 to 6
Outputs:
- attended: bfloat16 [16384, 8192], P('seq', 'tensor')
- grad_queries: bfloat16 [16384, 8192], P('seq', 'tensor')
- grad_features: bfloat16 [6144, 4096], P('seq', 'tensor')
The draws below stay inside these ranges and needn't reach their ends.
Inputs may be any that keep to these rules, and one draw needn't show every extreme that they name: `slot_image`: a permutation; each image id is encoded in a slot of its own aligned group of 4 slots. `image_range`: for a block among the tokens of seq index s: max(0, s - 2) <= first <= last <= s + 1; first == last means the block attends no image.
All inputs are finite; a program needn't handle non-finite values.
Results may differ from the reference program's by a relative error of at most 0.019.
Values may be sent and summed in bfloat16 or wider, within the bound.
A program may use at most 64 MiB of HBM per device.

```python
import jax
import jax.numpy as jnp
from jax import lax

D = 4096
HEADS = 64
KVH = 8
HD = 128
TILES = 4
TILE_ROWS = 24
TBLOCK = 64
GROUP = 4
LOOKBACK = 3
TOK_DEV = 256
TOKENS = 16384
NIMG = 64
ROWS = 96
NBLOCKS = 256
N_SEQ = 64
N_TENSOR = 8


def draw_slot_image(key, part):
    key = jax.random.fold_in(key, 11)
    slot_ids = jnp.arange(NIMG, dtype=jnp.int32)
    scores = jax.random.randint(key, (NIMG,), 0, 4096, dtype=jnp.int32) * NIMG + slot_ids
    ordered = jnp.argsort(slot_ids // GROUP * (4096 * NIMG) + scores, stable=True)
    return ordered.astype(jnp.int32)


def draw_image_range(key, part):
    key = jax.random.fold_in(key, 7)
    first_key, second_key = jax.random.split(key)
    blocks = jnp.arange(NBLOCKS, dtype=jnp.int32)
    shard_of = blocks // (TOK_DEV // TBLOCK)
    range_last = shard_of + 1 - jax.random.randint(first_key, (NBLOCKS,), 0, 2, dtype=jnp.int32)
    counted = jax.random.randint(second_key, (NBLOCKS,), 0, LOOKBACK + 1, dtype=jnp.int32)
    range_first = jnp.maximum(jnp.maximum(range_last - counted, shard_of - (LOOKBACK - 1)), 0)
    return jnp.stack([range_first, range_last], axis=1).astype(jnp.int32)


def place_ends(values, own_key, least, top_value):
    place = [jax.random.randint(jax.random.fold_in(own_key, axis), (), 0, length) for axis, length in enumerate(values.shape)]
    longest = values.shape.index(max(values.shape))
    beside = place[:longest] + [(place[longest] + 1) % values.shape[longest]] + place[longest + 1:]
    return values.at[tuple(place)].set(least).at[tuple(beside)].set(top_value)


def shard_levels(rng, dims, cuts, low, high):
    def one(dim, blocks):
        draws = jax.random.uniform(jax.random.fold_in(jax.random.fold_in(rng, 6), dim), (blocks,), jnp.float32, low / len(cuts), high / len(cuts))
        return jnp.repeat(jnp.exp(draws), dims[dim] // blocks).reshape((-1,) + (1,) * (len(dims) - dim - 1))

    level = one(*cuts[0])
    for cut in cuts[1:]:
        level = level * one(*cut)
    return level


def centred(own_key, shape, spread, reach, cuts=(), kind=jnp.bfloat16):
    drawn = spread * jax.random.normal(own_key, shape, jnp.float32)
    if cuts:
        drawn = drawn * shard_levels(own_key, shape, cuts, -0.22, 0.18)
    return jnp.clip(drawn, -reach, reach).astype(kind)


def setup_inputs(seed: int = 0) -> dict:
    key_of = jax.random.split(jax.random.key(seed), 11)
    queries = centred(key_of[0], (TOKENS, HEADS * HD), 1.0, 6.0, ((0, 64), (1, 8)))
    features = centred(key_of[1], (NIMG * ROWS, D), 1.0, 6.0, ((0, 64),))
    w_key = centred(key_of[2], (D, KVH * HD), D ** -0.5, 0.09375, ((1, 8),))
    w_value = centred(key_of[3], (D, KVH * HD), (D // 32) ** -0.5, 0.5, ((1, 8),))
    q_gain = jnp.clip(1.0 + 0.18 * jax.random.normal(key_of[4], (HD,), jnp.float32), 0.1, 1.9)
    k_gain = jnp.clip(1.0 + 0.18 * jax.random.normal(key_of[5], (HD,), jnp.float32), 0.1, 1.9)
    slot_image = draw_slot_image(jax.random.fold_in(key_of[10], 71), 0)
    image_tiles = place_ends(jax.random.randint(key_of[7], (NIMG,), 1, TILES + 1), jax.random.fold_in(key_of[7], 1), 1, TILES).astype(jnp.int32)
    image_range = draw_image_range(jax.random.fold_in(key_of[10], 71), 0)
    d_out = centred(key_of[9], (TOKENS, HEADS * HD), 1.0, 6.0, ((0, 64), (1, 8)))
    return {"queries": queries, "features": features, "w_key": w_key, "w_value": w_value, "q_gain": q_gain, "k_gain": k_gain, "slot_image": slot_image, "image_tiles": image_tiles, "image_range": image_range, "d_out": d_out}


def rms_scale(values, gain_vector):
    inverse = lax.rsqrt(lax.optimization_barrier(jnp.mean(values * values, axis=-1, keepdims=True)) + 1e-05)
    return (values * inverse * gain_vector, inverse)

def rms_back(values, inverse, gain_vector, upstream):
    scaled = gain_vector * upstream
    return inverse * scaled - values * inverse ** 3 * lax.optimization_barrier(jnp.mean(scaled * values, axis=-1, keepdims=True))

def rounded(values):
    return lax.optimization_barrier(values.astype(jnp.bfloat16)).astype(jnp.float32)

def reference(queries, features, w_key, w_value, q_gain, k_gain, slot_image, image_tiles, image_range, d_out):
    row_count = TILES * TILE_ROWS
    group_size = HEADS // KVH
    score_scale = HD ** (-0.5)
    per_shard = TOK_DEV // TBLOCK
    raw_keys = jnp.dot(features, w_key, preferred_element_type=jnp.float32).reshape(NIMG, row_count, KVH, HD)
    key_norm, key_inverse = rms_scale(raw_keys, k_gain)
    keys16 = lax.optimization_barrier(key_norm.astype(jnp.bfloat16))
    values16 = lax.optimization_barrier(jnp.dot(features, w_value, preferred_element_type=jnp.float32).astype(jnp.bfloat16)).reshape(NIMG, row_count, KVH, HD)
    keys_by_id = jnp.zeros_like(keys16).at[slot_image].set(keys16)
    values_by_id = jnp.zeros_like(values16).at[slot_image].set(values16)
    live_table = jnp.arange(row_count, dtype=jnp.int32)[None, :] < (image_tiles * TILE_ROWS)[:, None]

    def one_shard(state_pair, shard_index):
        grad_keys, grad_values = state_pair
        window_start = jnp.clip(shard_index - (LOOKBACK - 1), 0, NIMG - LOOKBACK).astype(jnp.int32)
        key_block = lax.dynamic_slice_in_dim(keys_by_id, window_start, LOOKBACK, 0).reshape(LOOKBACK * row_count, KVH, HD).astype(jnp.float32)
        value_block = lax.dynamic_slice_in_dim(values_by_id, window_start, LOOKBACK, 0).reshape(LOOKBACK * row_count, KVH, HD).astype(jnp.float32)
        live_keys = lax.dynamic_slice_in_dim(live_table, window_start, LOOKBACK, 0).reshape(LOOKBACK * row_count)
        key_ids = jnp.repeat(window_start + jnp.arange(LOOKBACK, dtype=jnp.int32), row_count)
        ranges = lax.dynamic_slice_in_dim(image_range, (shard_index * per_shard).astype(jnp.int32), per_shard, 0)
        range_first = jnp.repeat(ranges[:, 0], TBLOCK)
        range_last = jnp.repeat(ranges[:, 1], TBLOCK)
        key_mask = (key_ids[None, :] >= range_first[:, None]) & (key_ids[None, :] < range_last[:, None]) & live_keys[None, :]
        token_start = (shard_index * TOK_DEV).astype(jnp.int32)
        raw_query = lax.dynamic_slice_in_dim(queries, token_start, TOK_DEV, 0).astype(jnp.float32).reshape(TOK_DEV, KVH, group_size, HD)
        upstream = lax.dynamic_slice_in_dim(d_out, token_start, TOK_DEV, 0).astype(jnp.float32).reshape(TOK_DEV, KVH, group_size, HD)
        query_norm, query_inverse = rms_scale(raw_query, q_gain)
        query16 = rounded(query_norm)
        scores = jnp.einsum('tkgd,nkd->tkgn', query16, key_block) * score_scale
        exp_scores = jnp.where(key_mask[:, None, None, :], jnp.exp(scores), 0.0)
        denominator = lax.optimization_barrier(jnp.sum(exp_scores, axis=-1, keepdims=True))
        has_image = jnp.any(key_mask, axis=-1)[:, None, None, None]
        attn_weights = exp_scores / jnp.where(has_image, denominator, 1.0)
        weights16 = rounded(attn_weights)
        output_rows = jnp.einsum('tkgn,nkd->tkgd', weights16, value_block)
        grad_weights = jnp.einsum('tkgd,nkd->tkgn', upstream, value_block)
        row_delta = lax.optimization_barrier(jnp.sum(attn_weights * grad_weights, axis=-1, keepdims=True))
        grad_scores = rounded(attn_weights * (grad_weights - row_delta))
        grad_qnorm = jnp.einsum('tkgn,nkd->tkgd', grad_scores, key_block) * score_scale
        grad_query = rms_back(raw_query, query_inverse, q_gain, grad_qnorm)
        key_grad = (jnp.einsum('tkgn,tkgd->nkd', grad_scores, query16) * score_scale).reshape(LOOKBACK, row_count, KVH, HD)
        value_grad = jnp.einsum('tkgn,tkgd->nkd', weights16, upstream).reshape(LOOKBACK, row_count, KVH, HD)
        grad_keys = lax.dynamic_update_slice_in_dim(grad_keys, lax.dynamic_slice_in_dim(grad_keys, window_start, LOOKBACK, 0) + key_grad, window_start, 0)
        grad_values = lax.dynamic_update_slice_in_dim(grad_values, lax.dynamic_slice_in_dim(grad_values, window_start, LOOKBACK, 0) + value_grad, window_start, 0)
        shard_out = output_rows.astype(jnp.bfloat16).reshape(TOK_DEV, HEADS * HD)
        shard_grad = grad_query.astype(jnp.bfloat16).reshape(TOK_DEV, HEADS * HD)
        return ((grad_keys, grad_values), (shard_out, shard_grad))
    zero_grads = jnp.zeros((NIMG, row_count, KVH, HD), jnp.float32)
    (grad_keys, grad_values), (outputs, query_grads) = lax.scan(one_shard, (zero_grads, zero_grads), jnp.arange(N_SEQ, dtype=jnp.int32))
    attended = outputs.reshape(TOKENS, HEADS * HD)
    grad_queries = query_grads.reshape(TOKENS, HEADS * HD)
    slot_key_grad = grad_keys[slot_image]
    slot_value_grad = grad_values[slot_image]
    raw_grad = rms_back(raw_keys, key_inverse, k_gain, slot_key_grad).reshape(NIMG * row_count, KVH * HD).astype(jnp.bfloat16)
    value_grad16 = slot_value_grad.reshape(NIMG * row_count, KVH * HD).astype(jnp.bfloat16)
    heads_local = KVH // N_TENSOR
    contract = (((1,), (1,)), ((), ()))
    summed = jnp.zeros((NIMG * row_count, D), jnp.float32)
    for part_index in range(N_TENSOR):
        lower_col = part_index * heads_local * HD
        upper_col = lower_col + heads_local * HD
        head_term = lax.dot_general(raw_grad[:, lower_col:upper_col], w_key[:, lower_col:upper_col], contract, preferred_element_type=jnp.float32)
        head_term = head_term + lax.dot_general(value_grad16[:, lower_col:upper_col], w_value[:, lower_col:upper_col], contract, preferred_element_type=jnp.float32)
        summed = summed + rounded(head_term)
    return (attended, grad_queries, summed.astype(jnp.bfloat16))
```

```python
import functools

import jax
import jax.numpy as jnp
from jax import lax
from jax.experimental import pallas as pl
from jax.experimental.pallas import tpu as pltpu
from jax.sharding import PartitionSpec as P

TILE_ROWS = 24
GROUP = 4
LOOKBACK = 3
BF16 = jnp.bfloat16
F32 = jnp.float32
MESH = pl.DeviceIdType.MESH
LOG2E = 1.4426950408889634
HIDDEN = -1e30
W_CHUNKS = 4


def dot(a, b, contract):
    return lax.dot_general(a, b, (contract, ((), ())), preferred_element_type=F32)


def kernel(
    seq_count, tensor_count,
    q_hbm, f_hbm, wk_hbm, wv_hbm, qg_ref, kg_ref, slot_ref, tiles_ref, range_ref, do_hbm,
    att_hbm, gq_hbm, gf_hbm,
    f_v, w_v, q_v, do_v, att_v, gq_v, gf_v,
    raw_v, kv_in, kcat, q16_v, qt_v, inv_v, bias_v, p_v, ds_v,
    g_v, gsend, grecv, csend, crecv, rrecv, a_v,
    psend, precv, bsend, brecv,
    load_sem, store_sem, kv_send, kv_recv, relay_sem, g_send, g_recv, c_send, c_recv,
    rg_send, rg_recv, p_send, p_recv, b_send, b_recv,
):
    s = lax.axis_index("seq")
    t = lax.axis_index("tensor")
    g = s // GROUP
    m = s % GROUP
    base = g * GROUP
    chip = t // 2
    core = t % 2
    chips = tensor_count // 2
    groups = seq_count // GROUP
    rows, width = f_v.shape
    head = qg_ref.shape[1]
    toks = q_v.shape[0]
    heads = q_v.shape[1] // head
    scale = head ** (-0.5)
    has_next = g < groups - 1
    has_prev = g > 0
    partner = (s, t + 1 - 2 * core)

    step = width // W_CHUNKS
    loads = []
    for i in range(W_CHUNKS):
        part = pl.ds(i * step, step)
        loads.append([
            pltpu.make_async_copy(f_hbm.at[:, part], f_v.at[:, part], load_sem.at[3 * i]),
            pltpu.make_async_copy(wk_hbm.at[part, :], w_v.at[part, pl.ds(0, head)], load_sem.at[3 * i + 1]),
            pltpu.make_async_copy(wv_hbm.at[part, :], w_v.at[part, pl.ds(head, head)], load_sem.at[3 * i + 2]),
        ])
    q_load = pltpu.make_async_copy(q_hbm, q_v, load_sem.at[3 * W_CHUNKS])
    do_load = pltpu.make_async_copy(do_hbm, do_v, load_sem.at[3 * W_CHUNKS + 1])
    for group_loads in loads:
        for copy in group_loads:
            copy.start()
    q_load.start()
    do_load.start()

    barrier = pltpu.get_barrier_semaphore()

    def greet(device):
        pl.semaphore_signal(barrier, inc=1, device_id=device, device_id_type=MESH)

    for off in range(1, GROUP):
        greet((base + (m + off) % GROUP, t))
    greet(partner)
    for off in range(1, chips):
        greet((s, ((chip + off) % chips) * 2 + core))

    @pl.when(has_next)
    def _():
        greet((base + GROUP, t))

    @pl.when(has_next & (m == GROUP - 1))
    def _():
        greet((base + GROUP + 1, t))

    @pl.when(has_prev & (m == 0))
    def _():
        for e in range(GROUP):
            greet((base - GROUP + e, t))

    @pl.when(has_prev & (m == 1))
    def _():
        greet((base - 1, t))

    acc = jnp.zeros((rows, 2 * head), F32)
    for i in range(W_CHUNKS):
        for copy in loads[i]:
            copy.wait()
        part = slice(i * step, (i + 1) * step)
        acc = acc + dot(f_v[:, part], w_v[part, :], ((1,), (0,)))
    raw = acc[:, :head]
    raw_v[...] = raw
    kinv = lax.rsqrt(jnp.mean(raw * raw, axis=-1, keepdims=True) + 1e-05)
    kv_in[m, :, :head] = (raw * kinv * kg_ref[...]).astype(BF16)
    kv_in[m, :, head:] = acc[:, head:].astype(BF16)

    peers = (
        GROUP - 1 + chips
        + jnp.where(has_next, 1, 0)
        + jnp.where(has_next & (m == GROUP - 1), 1, 0)
        + jnp.where(has_prev & (m == 0), GROUP, 0)
        + jnp.where(has_prev & (m == 1), 1, 0)
    )
    pl.semaphore_wait(barrier, peers)

    def remote(src, dst, send, recv, device):
        return pltpu.make_async_remote_copy(
            src_ref=src, dst_ref=dst, send_sem=send, recv_sem=recv,
            device_id=device, device_id_type=MESH,
        )

    def kv_cross():
        return remote(
            kv_in.at[m], kv_in.at[GROUP + m], kv_send.at[GROUP - 1], kv_recv.at[GROUP + m],
            (base + GROUP, t),
        )

    def kv_group(off):
        return remote(
            kv_in.at[m], kv_in.at[m], kv_send.at[off - 1], kv_recv.at[m],
            (base + (m + off) % GROUP, t),
        )

    def kv_arrived(slot):
        pltpu.make_async_copy(kv_in.at[slot], kv_in.at[slot], kv_recv.at[slot]).wait()

    @pl.when(has_next)
    def _():
        kv_cross().start()

    for off in range(1, GROUP):
        kv_group(off).start()

    q_load.wait()
    for h in range(heads):
        cols = slice(h * head, (h + 1) * head)
        x = q_v[:, cols].astype(F32)
        inv = lax.rsqrt(jnp.mean(x * x, axis=-1, keepdims=True) + 1e-05)
        inv_v[h] = jnp.broadcast_to(inv, (toks, head))
        normed = (x * inv * qg_ref[...]).astype(BF16)
        q16_v[:, cols] = normed
        qt_v[h] = normed.astype(F32).T.astype(BF16)

    blocks = range_ref.shape[0]
    per_block = toks // blocks
    block_of = lax.broadcasted_iota(jnp.int32, (1, toks), 1) // per_block
    row_of = lax.broadcasted_iota(jnp.int32, (rows, toks), 0)
    for j in range(LOOKBACK):
        image = s - (LOOKBACK - 1) + j
        live = tiles_ref[jnp.maximum(image, 0)] * TILE_ROWS
        limit = jnp.zeros((1, toks), jnp.int32)
        for b in range(blocks):
            seen = (range_ref[b, 0] <= image) & (image < range_ref[b, 1])
            limit = jnp.where(block_of == b, jnp.where(seen, live, 0), limit)
        bias_v[j * rows:(j + 1) * rows, :] = jnp.where(row_of < limit, 0.0, HIDDEN)
    do_load.wait()

    for off in range(1, GROUP):
        kv_arrived((m + off) % GROUP)
    ids = [slot_ref[base + e] for e in range(GROUP)]
    for j in range(LOOKBACK):
        image = s - (LOOKBACK - 1) + j
        chosen = jnp.zeros((rows, 2 * head), BF16)
        for e in range(GROUP):
            chosen = jnp.where(ids[e] == image, kv_in[e], chosen)
        kcat[j * rows:(j + 1) * rows, :] = chosen

    last = pl.ds((LOOKBACK - 1) * rows, rows)

    def kv_relay():
        return remote(
            kcat.at[last], kv_in.at[GROUP], relay_sem, kv_recv.at[GROUP], (base + GROUP + 1, t)
        )

    @pl.when(has_next & (m == GROUP - 1))
    def _():
        kv_relay().start()

    @pl.when(has_prev & (m == 0))
    def _():
        for e in range(GROUP):
            kv_arrived(GROUP + e)
        for j in range(LOOKBACK - 1):
            image = s - (LOOKBACK - 1) + j
            chosen = jnp.zeros((rows, 2 * head), BF16)
            for e in range(GROUP):
                chosen = jnp.where(slot_ref[base - GROUP + e] == image, kv_in[GROUP + e], chosen)
            kcat[j * rows:(j + 1) * rows, :] = chosen

    @pl.when(has_prev & (m == 1))
    def _():
        kv_arrived(GROUP)
        kcat[:rows, :] = kv_in[GROUP]

    keys = kcat[:, :head]
    values = kcat[:, head:]
    for h in range(heads):
        cols = slice(h * head, (h + 1) * head)
        scores = dot(keys, qt_v[h], ((1,), (0,)))
        e = jnp.exp2(scores * (scale * LOG2E) + bias_v[...])
        total = jnp.sum(e, axis=0, keepdims=True)
        p = e * jnp.where(total > 0.0, 1.0 / total, 0.0)
        p_v[h] = p.astype(BF16)
        dp = dot(values, do_v[:, cols], ((1,), (1,)))
        delta = jnp.sum(p * dp, axis=0, keepdims=True)
        ds_v[h] = (p * (dp - delta)).astype(BF16)

    for j in range(LOOKBACK):
        part = slice(j * rows, (j + 1) * rows)
        dk = jnp.zeros((rows, head), F32)
        dv = jnp.zeros((rows, head), F32)
        for h in range(heads):
            cols = slice(h * head, (h + 1) * head)
            dk = dk + dot(ds_v[h, part, :], q16_v[:, cols], ((1,), (0,)))
            dv = dv + dot(p_v[h, part, :], do_v[:, cols], ((1,), (0,)))
        g_v[j, :, :head] = dk * scale
        g_v[j, :, head:] = dv

    def for_slot(image_id, count):
        total = jnp.zeros((rows, 2 * head), F32)
        for j in range(count):
            total = jnp.where(image_id == s - (LOOKBACK - 1) + j, g_v[j], total)
        return total

    def cross_back(e):
        return remote(csend.at[e], crecv, c_send.at[e], c_recv, (base - GROUP + e, t))

    def relay_back():
        return remote(csend.at[0], rrecv, rg_send, rg_recv, (base - 1, t))

    @pl.when(has_prev & (m == 0))
    def _():
        for e in range(GROUP):
            csend[e] = for_slot(slot_ref[base - GROUP + e], LOOKBACK - 1).astype(BF16)
            cross_back(e).start()

    @pl.when(has_prev & (m == 1))
    def _():
        csend[0] = g_v[0].astype(BF16)
        relay_back().start()

    @pl.when(has_next & (m == GROUP - 1))
    def _():
        pltpu.make_async_copy(rrecv, rrecv, rg_recv).wait()
        g_v[LOOKBACK - 1] = g_v[LOOKBACK - 1] + rrecv[...].astype(F32)

    def group_back(off):
        return remote(
            gsend.at[off - 1], grecv.at[off - 1], g_send.at[off - 1], g_recv.at[off - 1],
            (base + (m + off) % GROUP, t),
        )

    for off in range(1, GROUP):
        gsend[off - 1] = for_slot(slot_ref[base + (m + off) % GROUP], LOOKBACK).astype(BF16)
        group_back(off).start()

    for h in range(heads):
        cols = slice(h * head, (h + 1) * head)
        att_v[:, cols] = dot(p_v[h], values, ((0,), (0,))).astype(BF16)
        x = q_v[:, cols].astype(F32)
        inv = inv_v[h]
        up = dot(ds_v[h], keys, ((0,), (0,))) * (qg_ref[...] * scale)
        mean = jnp.mean(up * x, axis=-1, keepdims=True)
        gq_v[:, cols] = (inv * up - x * (inv * inv * inv) * mean).astype(BF16)
    att_store = pltpu.make_async_copy(att_v, att_hbm, store_sem.at[0])
    gq_store = pltpu.make_async_copy(gq_v, gq_hbm, store_sem.at[1])
    att_store.start()
    gq_store.start()

    mine = for_slot(slot_ref[s], LOOKBACK)
    g_v[0] = mine
    for off in range(1, GROUP):
        group_back(off).wait_recv()
        g_v[0] = g_v[0] + grecv[off - 1].astype(F32)

    @pl.when(has_next)
    def _():
        pltpu.make_async_copy(crecv, crecv, c_recv).wait()
        g_v[0] = g_v[0] + crecv[...].astype(F32)

    raw = raw_v[...]
    kinv = lax.rsqrt(jnp.mean(raw * raw, axis=-1, keepdims=True) + 1e-05)
    up = g_v[0, :, :head] * kg_ref[...]
    mean = jnp.mean(up * raw, axis=-1, keepdims=True)
    a_v[:, :head] = (kinv * up - raw * (kinv * kinv * kinv) * mean).astype(BF16)
    a_v[:, head:] = g_v[0, :, head:].astype(BF16)

    out_cols = gf_v.shape[1]

    def term(owner):
        part = pl.ds(pl.multiple_of(owner * out_cols, out_cols), out_cols)
        return dot(a_v[...], w_v[part, :], ((1,), (1,)))

    def to_partner(i):
        return remote(psend.at[i], precv.at[i], p_send.at[i], p_recv.at[i], partner)

    def to_chip(i):
        return remote(
            bsend.at[i - 1], brecv.at[i - 1], b_send.at[i - 1], b_recv.at[i - 1],
            (s, ((chip + i) % chips) * 2 + core),
        )

    order = list(range(1, chips)) + [0]
    for i in order:
        psend[i] = term(((chip + i) % chips) * 2 + 1 - core).astype(BF16)
        to_partner(i).start()
    for i in order:
        own = term(((chip + i) % chips) * 2 + core).astype(BF16).astype(F32)
        to_partner(i).wait_recv()
        both = own + precv[i].astype(F32)
        if i:
            bsend[i - 1] = both.astype(BF16)
            to_chip(i).start()
    for i in range(1, chips):
        to_chip(i).wait_recv()
        both = both + brecv[i - 1].astype(F32)
    gf_v[...] = both.astype(BF16)
    gf_store = pltpu.make_async_copy(gf_v, gf_hbm, store_sem.at[2])
    gf_store.start()

    for off in range(1, GROUP):
        kv_group(off).wait_send()
        group_back(off).wait_send()

    @pl.when(has_next)
    def _():
        kv_cross().wait_send()

    @pl.when(has_next & (m == GROUP - 1))
    def _():
        kv_relay().wait_send()

    @pl.when(has_prev & (m == 0))
    def _():
        for e in range(GROUP):
            cross_back(e).wait_send()

    @pl.when(has_prev & (m == 1))
    def _():
        relay_back().wait_send()

    for i in range(chips):
        to_partner(i).wait_send()
    for i in range(1, chips):
        to_chip(i).wait_send()
    att_store.wait()
    gq_store.wait()
    gf_store.wait()


def local(
    queries, features, w_key, w_value, q_gain, k_gain, slot_image, image_tiles, image_range, d_out
):
    seq_count = lax.axis_size("seq")
    tensor_count = lax.axis_size("tensor")
    chips = tensor_count // 2
    toks, q_cols = queries.shape
    rows, width = features.shape
    head = q_gain.shape[0]
    heads = q_cols // head
    keys = LOOKBACK * rows
    out_cols = width // tensor_count
    dma = pltpu.SemaphoreType.DMA
    any_space = pl.BlockSpec(memory_space=pl.ANY)
    vmem = pl.BlockSpec(memory_space=pltpu.VMEM)
    smem = pl.BlockSpec(memory_space=pltpu.SMEM)
    scratch = [
        pltpu.VMEM((rows, width), BF16),
        pltpu.VMEM((width, 2 * head), BF16),
        pltpu.VMEM((toks, q_cols), BF16),
        pltpu.VMEM((toks, q_cols), BF16),
        pltpu.VMEM((toks, q_cols), BF16),
        pltpu.VMEM((toks, q_cols), BF16),
        pltpu.VMEM((rows, out_cols), BF16),
        pltpu.VMEM((rows, head), F32),
        pltpu.VMEM((2 * GROUP, rows, 2 * head), BF16),
        pltpu.VMEM((keys, 2 * head), BF16),
        pltpu.VMEM((toks, q_cols), BF16),
        pltpu.VMEM((heads, head, toks), BF16),
        pltpu.VMEM((heads, toks, head), F32),
        pltpu.VMEM((keys, toks), F32),
        pltpu.VMEM((heads, keys, toks), BF16),
        pltpu.VMEM((heads, keys, toks), BF16),
        pltpu.VMEM((LOOKBACK, rows, 2 * head), F32),
        pltpu.VMEM((GROUP - 1, rows, 2 * head), BF16),
        pltpu.VMEM((GROUP - 1, rows, 2 * head), BF16),
        pltpu.VMEM((GROUP, rows, 2 * head), BF16),
        pltpu.VMEM((rows, 2 * head), BF16),
        pltpu.VMEM((rows, 2 * head), BF16),
        pltpu.VMEM((rows, 2 * head), BF16),
        pltpu.VMEM((chips, rows, out_cols), BF16),
        pltpu.VMEM((chips, rows, out_cols), BF16),
        pltpu.VMEM((chips - 1, rows, out_cols), BF16),
        pltpu.VMEM((chips - 1, rows, out_cols), BF16),
        dma((3 * W_CHUNKS + 2,)),
        dma((3,)),
        dma((GROUP,)),
        dma((2 * GROUP,)),
        dma,
        dma((GROUP - 1,)),
        dma((GROUP - 1,)),
        dma((GROUP,)),
        dma,
        dma,
        dma,
        dma((chips,)),
        dma((chips,)),
        dma((chips - 1,)),
        dma((chips - 1,)),
    ]
    return pl.pallas_call(
        functools.partial(kernel, seq_count, tensor_count),
        out_shape=(
            jax.ShapeDtypeStruct((toks, q_cols), BF16),
            jax.ShapeDtypeStruct((toks, q_cols), BF16),
            jax.ShapeDtypeStruct((rows, out_cols), BF16),
        ),
        in_specs=[any_space] * 4 + [vmem] * 2 + [smem] * 3 + [any_space],
        out_specs=(any_space,) * 3,
        scratch_shapes=scratch,
        compiler_params=pltpu.CompilerParams(
            collective_id=0, has_side_effects=True, vmem_limit_bytes=48 * 1024 * 1024
        ),
        cost_estimate=pl.CostEstimate(
            flops=1_300_000_000, bytes_accessed=5_500_000, transcendentals=600_000
        ),
    )(
        queries, features, w_key, w_value, q_gain.reshape(1, head), k_gain.reshape(1, head),
        slot_image, image_tiles, image_range, d_out,
    )


def solution(mesh):
    in_specs = (
        P("seq", "tensor"),
        P("seq", None),
        P(None, "tensor"),
        P(None, "tensor"),
        P(),
        P(),
        P(),
        P(),
        P("seq", None),
        P("seq", "tensor"),
    )
    out_specs = (P("seq", "tensor"), P("seq", "tensor"), P("seq", "tensor"))
    return jax.shard_map(local, mesh=mesh, in_specs=in_specs, out_specs=out_specs, check_vma=False)
```

```python
import functools

import jax
import jax.numpy as jnp
from jax import lax
from jax.experimental import pallas as pl
from jax.experimental.pallas import tpu as pltpu
from jax.sharding import PartitionSpec as P

TILE_ROWS = 24
GROUP = 4
LOOKBACK = 3
BF16 = jnp.bfloat16
F32 = jnp.float32
MESH = pl.DeviceIdType.MESH
LOG2E = 1.4426950408889634
HIDDEN = -1e30
W_CHUNKS = 4


def dot(a, b, contract):
    return lax.dot_general(a, b, (contract, ((), ())), preferred_element_type=F32)


def kernel(
    seq_count, tensor_count,
    q_hbm, f_hbm, wk_hbm, wv_hbm, qg_hbm, kg_hbm, slot_hbm, tiles_hbm, range_hbm, do_hbm,
    att_hbm, gq_hbm, gf_hbm,
    qg_ref, kg_ref, slot_ref, tiles_ref, range_ref,
    f_v, w_v, q_v, do_v, att_v, gq_v, gf_v,
    raw_v, kv_in, kcat, q16_v, qt_v, inv_v, bias_v, p_v, ds_v,
    g_v, gsend, grecv, csend, crecv, a_v,
    psend, precv, bsend, brecv, sum_v,
    small_sem, load_sem, store_sem, kv_send, kv_recv, g_send, g_recv, c_send, c_recv,
    p_send, p_recv, b_send, b_recv,
):
    s = lax.axis_index("seq")
    t = lax.axis_index("tensor")
    g = s // GROUP
    m = s % GROUP
    base = g * GROUP
    chip = t // 2
    core = t % 2
    chips = tensor_count // 2
    groups = seq_count // GROUP
    rows, width = f_v.shape
    head = qg_ref.shape[1]
    toks = q_v.shape[0]
    heads = q_v.shape[1] // head
    scale = head ** (-0.5)
    has_next = g < groups - 1
    has_prev = g > 0
    follows = has_prev & (m < 2)
    inner = (chip % 3 + 1) // 2
    partner = (s, t + 1 - 2 * core)

    pending = []

    def finish():
        for wait in pending:
            wait()

    def when_done(condition, waits):
        def wait_all():
            @pl.when(condition)
            def _():
                for wait in waits:
                    wait()

        pending.append(wait_all)

    barrier = pltpu.get_barrier_semaphore()

    def greet(device):
        pl.semaphore_signal(barrier, inc=1, device_id=device, device_id_type=MESH)

    @pl.when(has_next)
    def _():
        greet((base + GROUP, t))
        greet((base + GROUP + 1, t))

    @pl.when(follows)
    def _():
        for e in range(GROUP):
            greet((base - GROUP + e, t))

    for off in range(1, GROUP):
        greet((base + (m + off) % GROUP, t))
    greet(partner)
    for off in range(1, chips):
        greet((s, ((chip + off) % chips) * 2 + core))

    step = width // W_CHUNKS
    loads = []
    for i in range(W_CHUNKS):
        part = pl.ds(i * step, step)
        loads.append([
            pltpu.make_async_copy(f_hbm.at[:, part], f_v.at[:, part], load_sem.at[3 * i]),
            pltpu.make_async_copy(wk_hbm.at[part, :], w_v.at[part, pl.ds(0, head)], load_sem.at[3 * i + 1]),
            pltpu.make_async_copy(wv_hbm.at[part, :], w_v.at[part, pl.ds(head, head)], load_sem.at[3 * i + 2]),
        ])
    q_load = pltpu.make_async_copy(q_hbm, q_v, load_sem.at[3 * W_CHUNKS])
    do_load = pltpu.make_async_copy(do_hbm, do_v, load_sem.at[3 * W_CHUNKS + 1])
    small_loads = [
        pltpu.make_async_copy(src, dst, small_sem.at[i])
        for i, (src, dst) in enumerate([
            (kg_hbm, kg_ref), (qg_hbm, qg_ref), (slot_hbm, slot_ref), (tiles_hbm, tiles_ref),
            (range_hbm, range_ref),
        ])
    ]
    small_loads[0].start()
    for group_loads in loads:
        for copy in group_loads:
            copy.start()
    q_load.start()
    do_load.start()
    for copy in small_loads[1:]:
        copy.start()

    acc = jnp.zeros((rows, 2 * head), F32)
    for i in range(W_CHUNKS):
        for copy in loads[i]:
            copy.wait()
        part = slice(i * step, (i + 1) * step)
        acc = acc + dot(f_v[:, part], w_v[part, :], ((1,), (0,)))
    small_loads[0].wait()
    raw = acc[:, :head]
    raw_v[...] = raw
    kinv = lax.rsqrt(jnp.mean(raw * raw, axis=-1, keepdims=True) + 1e-05)
    kv_in[m, :, :head] = (raw * kinv * kg_ref[...]).astype(BF16)
    kv_in[m, :, head:] = acc[:, head:].astype(BF16)

    peers = (
        GROUP - 1 + chips
        + jnp.where(has_next, 2, 0)
        + jnp.where(follows, GROUP, 0)
    )
    pl.semaphore_wait(barrier, peers)

    def remote(src, dst, send, recv, device):
        return pltpu.make_async_remote_copy(
            src_ref=src, dst_ref=dst, send_sem=send, recv_sem=recv,
            device_id=device, device_id_type=MESH,
        )

    def kv_cross(i):
        return remote(
            kv_in.at[m], kv_in.at[GROUP + m], kv_send.at[GROUP - 1 + i], kv_recv.at[GROUP + m],
            (base + GROUP + i, t),
        )

    def kv_group(off):
        return remote(
            kv_in.at[m], kv_in.at[m], kv_send.at[off - 1], kv_recv.at[m],
            (base + (m + off) % GROUP, t),
        )

    def kv_arrived(slot):
        pltpu.make_async_copy(kv_in.at[slot], kv_in.at[slot], kv_recv.at[slot]).wait()

    @pl.when(has_next)
    def _():
        for i in range(2):
            kv_cross(i).start()

    when_done(has_next, [lambda i=i: kv_cross(i).wait_send() for i in range(2)])

    for off in range(1, GROUP):
        kv_group(off).start()
        pending.append(lambda off=off: kv_group(off).wait_send())

    q_load.wait()
    for copy in small_loads[1:]:
        copy.wait()
    for h in range(heads):
        cols = slice(h * head, (h + 1) * head)
        x = q_v[:, cols].astype(F32)
        inv = lax.rsqrt(jnp.mean(x * x, axis=-1, keepdims=True) + 1e-05)
        inv_v[h] = jnp.broadcast_to(inv, (toks, head))
        normed = (x * inv * qg_ref[...]).astype(BF16)
        q16_v[:, cols] = normed
        qt_v[h] = normed.astype(F32).T.astype(BF16)

    blocks = range_ref.shape[1]
    per_block = toks // blocks
    block_of = lax.broadcasted_iota(jnp.int32, (1, toks), 1) // per_block
    row_of = lax.broadcasted_iota(jnp.int32, (rows, toks), 0)
    for j in range(LOOKBACK):
        image = s - (LOOKBACK - 1) + j
        live = tiles_ref[jnp.maximum(image, 0)] * TILE_ROWS
        limit = jnp.zeros((1, toks), jnp.int32)
        for b in range(blocks):
            seen = (range_ref[0, b] <= image) & (image < range_ref[1, b])
            limit = jnp.where(block_of == b, jnp.where(seen, live, 0), limit)
        bias_v[j * rows:(j + 1) * rows, :] = jnp.where(row_of < limit, 0.0, HIDDEN)
    do_load.wait()

    for off in range(1, GROUP):
        kv_arrived((m + off) % GROUP)
    ids = [slot_ref[base + e] for e in range(GROUP)]
    for j in range(LOOKBACK):
        image = s - (LOOKBACK - 1) + j
        chosen = jnp.zeros((rows, 2 * head), BF16)
        for e in range(GROUP):
            chosen = jnp.where(ids[e] == image, kv_in[e], chosen)
        kcat[j * rows:(j + 1) * rows, :] = chosen

    @pl.when(follows)
    def _():
        for e in range(GROUP):
            kv_arrived(GROUP + e)
        for j in range(LOOKBACK - 1):
            image = s - (LOOKBACK - 1) + j
            chosen = kcat[j * rows:(j + 1) * rows, :]
            for e in range(GROUP):
                chosen = jnp.where(slot_ref[base - GROUP + e] == image, kv_in[GROUP + e], chosen)
            kcat[j * rows:(j + 1) * rows, :] = chosen

    keys = kcat[:, :head]
    values = kcat[:, head:]
    for h in range(heads):
        cols = slice(h * head, (h + 1) * head)
        scores = dot(keys, qt_v[h], ((1,), (0,)))
        e = jnp.exp2(scores * (scale * LOG2E) + bias_v[...])
        total = jnp.sum(e, axis=0, keepdims=True)
        p = e * jnp.where(total > 0.0, 1.0 / total, 0.0)
        p_v[h] = p.astype(BF16)
        dp = dot(values, do_v[:, cols], ((1,), (1,)))
        delta = jnp.sum(p * dp, axis=0, keepdims=True)
        ds_v[h] = (p * (dp - delta)).astype(BF16)

    def image_grads(j):
        part = slice(j * rows, (j + 1) * rows)
        dk = jnp.zeros((rows, head), F32)
        dv = jnp.zeros((rows, head), F32)
        for h in range(heads):
            cols = slice(h * head, (h + 1) * head)
            dk = dk + dot(ds_v[h, part, :], q16_v[:, cols], ((1,), (0,)))
            dv = dv + dot(p_v[h, part, :], do_v[:, cols], ((1,), (0,)))
        g_v[j, :, :head] = dk * scale
        g_v[j, :, head:] = dv

    def for_slot(image_id, count):
        total = jnp.zeros((rows, 2 * head), F32)
        for j in range(count):
            total = jnp.where(image_id == s - (LOOKBACK - 1) + j, g_v[j], total)
        return total

    for j in range(LOOKBACK - 1):
        image_grads(j)

    def cross_back(e):
        return remote(csend.at[e], crecv.at[m], c_send.at[e], c_recv.at[m], (base - GROUP + e, t))

    @pl.when(follows)
    def _():
        for e in range(GROUP):
            csend[e] = for_slot(slot_ref[base - GROUP + e], LOOKBACK - 1).astype(BF16)
            cross_back(e).start()

    when_done(follows, [lambda e=e: cross_back(e).wait_send() for e in range(GROUP)])
    image_grads(LOOKBACK - 1)

    def group_back(off):
        return remote(
            gsend.at[off - 1], grecv.at[off - 1], g_send.at[off - 1], g_recv.at[off - 1],
            (base + (m + off) % GROUP, t),
        )

    for off in range(1, GROUP):
        gsend[off - 1] = for_slot(slot_ref[base + (m + off) % GROUP], LOOKBACK).astype(BF16)
        group_back(off).start()
        pending.append(lambda off=off: group_back(off).wait_send())

    for h in range(heads):
        cols = slice(h * head, (h + 1) * head)
        att_v[:, cols] = dot(p_v[h], values, ((0,), (0,))).astype(BF16)
        x = q_v[:, cols].astype(F32)
        inv = inv_v[h]
        up = dot(ds_v[h], keys, ((0,), (0,))) * (qg_ref[...] * scale)
        mean = jnp.mean(up * x, axis=-1, keepdims=True)
        gq_v[:, cols] = (inv * up - x * (inv * inv * inv) * mean).astype(BF16)
    att_store = pltpu.make_async_copy(att_v, att_hbm, store_sem.at[0])
    gq_store = pltpu.make_async_copy(gq_v, gq_hbm, store_sem.at[1])
    att_store.start()
    gq_store.start()
    pending.extend([att_store.wait, gq_store.wait])

    mine = for_slot(slot_ref[s], LOOKBACK)
    g_v[0] = mine
    for off in range(1, GROUP):
        group_back(off).wait_recv()
        g_v[0] = g_v[0] + grecv[off - 1].astype(F32)

    @pl.when(has_next)
    def _():
        for i in range(2):
            pltpu.make_async_copy(crecv.at[i], crecv.at[i], c_recv.at[i]).wait()
            g_v[0] = g_v[0] + crecv[i].astype(F32)

    raw = raw_v[...]
    kinv = lax.rsqrt(jnp.mean(raw * raw, axis=-1, keepdims=True) + 1e-05)
    up = g_v[0, :, :head] * kg_ref[...]
    mean = jnp.mean(up * raw, axis=-1, keepdims=True)
    a_v[:, :head] = (kinv * up - raw * (kinv * kinv * kinv) * mean).astype(BF16)
    a_v[:, head:] = g_v[0, :, head:].astype(BF16)

    out_cols = gf_v.shape[1]

    def term(owner):
        part = pl.ds(pl.multiple_of(owner * out_cols, out_cols), out_cols)
        return dot(a_v[...], w_v[part, :], ((1,), (1,)))

    def to_partner(i):
        return remote(psend.at[i], precv.at[i], p_send.at[i], p_recv.at[i], partner)

    mate = chip + (1 - 2 * (chip % 2))
    far_mate = chips - 1 - mate
    far_same = chips - 1 - chip
    order = [
        inner * far_same + (1 - inner) * far_same,
        inner * mate + (1 - inner) * far_mate,
        inner * far_mate + (1 - inner) * mate,
        chip,
    ]
    target = [inner * order[0] + (1 - inner) * mate, order[1], order[2]]
    landing = [3 - 2 * inner, 2 - 2 * inner, inner]

    def to_chip(i):
        return remote(
            bsend.at[i], brecv.at[landing[i]], b_send.at[i], b_recv.at[landing[i]],
            (s, target[i] * 2 + core),
        )

    def landed(slot):
        pltpu.make_async_copy(brecv.at[slot], brecv.at[slot], b_recv.at[slot]).wait()
        return brecv[slot].astype(F32)

    for i in range(chips):
        psend[i] = term(order[i] * 2 + 1 - core).astype(BF16)
        to_partner(i).start()
        pending.append(lambda i=i: to_partner(i).wait_send())
    for i in (0, 1, 3, 2):
        own = term(order[i] * 2 + core).astype(BF16).astype(F32)
        to_partner(i).wait_recv()
        both = own + precv[i].astype(F32)
        if i == 3:
            sum_v[...] = both
            continue
        bsend[i] = both.astype(BF16)
        if i == 2:
            @pl.when(inner == 1)
            def _():
                bsend[2] = (bsend[2].astype(F32) + landed(3)).astype(BF16)
        to_chip(i).start()
        pending.append(lambda i=i: to_chip(i).wait_send())
    sum_v[...] = sum_v[...] + landed(0)

    @pl.when(inner == 1)
    def _():
        sum_v[...] = sum_v[...] + landed(2)

    both = sum_v[...] + landed(1)
    gf_v[...] = both.astype(BF16)
    gf_store = pltpu.make_async_copy(gf_v, gf_hbm, store_sem.at[2])
    gf_store.start()
    pending.append(gf_store.wait)

    finish()


def local(
    queries, features, w_key, w_value, q_gain, k_gain, slot_image, image_tiles, image_range, d_out
):
    seq_count = lax.axis_size("seq")
    tensor_count = lax.axis_size("tensor")
    chips = tensor_count // 2
    toks, q_cols = queries.shape
    rows, width = features.shape
    head = q_gain.shape[0]
    heads = q_cols // head
    keys = LOOKBACK * rows
    out_cols = width // tensor_count
    dma = pltpu.SemaphoreType.DMA
    any_space = pl.BlockSpec(memory_space=pl.ANY)
    hbm = pl.BlockSpec(memory_space=pltpu.HBM)
    scratch = [
        pltpu.VMEM((1, head), F32),
        pltpu.VMEM((1, head), F32),
        pltpu.SMEM(slot_image.shape, jnp.int32),
        pltpu.SMEM(image_tiles.shape, jnp.int32),
        pltpu.SMEM(image_range.shape[::-1], jnp.int32),
        pltpu.VMEM((rows, width), BF16),
        pltpu.VMEM((width, 2 * head), BF16),
        pltpu.VMEM((toks, q_cols), BF16),
        pltpu.VMEM((toks, q_cols), BF16),
        pltpu.VMEM((toks, q_cols), BF16),
        pltpu.VMEM((toks, q_cols), BF16),
        pltpu.VMEM((rows, out_cols), BF16),
        pltpu.VMEM((rows, head), F32),
        pltpu.VMEM((2 * GROUP, rows, 2 * head), BF16),
        pltpu.VMEM((keys, 2 * head), BF16),
        pltpu.VMEM((toks, q_cols), BF16),
        pltpu.VMEM((heads, head, toks), BF16),
        pltpu.VMEM((heads, toks, head), F32),
        pltpu.VMEM((keys, toks), F32),
        pltpu.VMEM((heads, keys, toks), BF16),
        pltpu.VMEM((heads, keys, toks), BF16),
        pltpu.VMEM((LOOKBACK, rows, 2 * head), F32),
        pltpu.VMEM((GROUP - 1, rows, 2 * head), BF16),
        pltpu.VMEM((GROUP - 1, rows, 2 * head), BF16),
        pltpu.VMEM((GROUP, rows, 2 * head), BF16),
        pltpu.VMEM((2, rows, 2 * head), BF16),
        pltpu.VMEM((rows, 2 * head), BF16),
        pltpu.VMEM((chips, rows, out_cols), BF16),
        pltpu.VMEM((chips, rows, out_cols), BF16),
        pltpu.VMEM((chips - 1, rows, out_cols), BF16),
        pltpu.VMEM((chips, rows, out_cols), BF16),
        pltpu.VMEM((rows, out_cols), F32),
        dma((5,)),
        dma((3 * W_CHUNKS + 2,)),
        dma((3,)),
        dma((GROUP + 1,)),
        dma((2 * GROUP,)),
        dma((GROUP - 1,)),
        dma((GROUP - 1,)),
        dma((GROUP,)),
        dma((2,)),
        dma((chips,)),
        dma((chips,)),
        dma((chips - 1,)),
        dma((chips,)),
    ]
    return pl.pallas_call(
        functools.partial(kernel, seq_count, tensor_count),
        out_shape=(
            jax.ShapeDtypeStruct((toks, q_cols), BF16),
            jax.ShapeDtypeStruct((toks, q_cols), BF16),
            jax.ShapeDtypeStruct((rows, out_cols), BF16),
        ),
        in_specs=[hbm] * 10,
        out_specs=(any_space,) * 3,
        scratch_shapes=scratch,
        compiler_params=pltpu.CompilerParams(
            collective_id=0, has_side_effects=True, vmem_limit_bytes=105 * 512 * 1024
        ),
        cost_estimate=pl.CostEstimate(
            flops=1_300_000_000, bytes_accessed=5_500_000, transcendentals=600_000
        ),
    )(
        queries, features, w_key, w_value, q_gain.reshape(1, head), k_gain.reshape(1, head),
        slot_image, image_tiles, image_range.T, d_out,
    )


def solution(mesh):
    in_specs = (
        P("seq", "tensor"),
        P("seq", None),
        P(None, "tensor"),
        P(None, "tensor"),
        P(),
        P(),
        P(),
        P(),
        P("seq", None),
        P("seq", "tensor"),
    )
    out_specs = (P("seq", "tensor"), P("seq", "tensor"), P("seq", "tensor"))
    return jax.shard_map(local, mesh=mesh, in_specs=in_specs, out_specs=out_specs, check_vma=False)
```

```python
import functools

import jax
import jax.numpy as jnp
from jax import lax
from jax.experimental import pallas as pl
from jax.experimental.pallas import tpu as pltpu
from jax.sharding import PartitionSpec as P

TILE_ROWS = 24
GROUP = 4
LOOKBACK = 3
BF16 = jnp.bfloat16
F32 = jnp.float32
MESH = pl.DeviceIdType.MESH
LOG2E = 1.4426950408889634
HIDDEN = -1e30
W_CHUNKS = 4


def dot(a, b, contract):
    return lax.dot_general(a, b, (contract, ((), ())), preferred_element_type=F32)


def kernel(
    seq_count, tensor_count,
    q_hbm, f_hbm, wk_hbm, wv_hbm, qg_hbm, kg_hbm, slot_hbm, tiles_hbm, range_hbm, do_hbm,
    att_hbm, gq_hbm, gf_hbm,
    qg_ref, kg_ref, slot_ref, tiles_ref, range_ref,
    f_v, w_v, q_v, do_v, att_v, gq_v, gf_v,
    raw_v, kv_in, kcat, q16_v, qt_v, inv_v, bias_v, p_v, ds_v,
    g_v, gsend, grecv, csend, crecv, a_v,
    psend, precv, bsend, brecv, sum_v,
    small_sem, load_sem, store_sem, kv_send, kv_recv, g_send, g_recv, c_send, c_recv,
    p_send, p_recv, b_send, b_recv,
):
    s = lax.axis_index("seq")
    t = lax.axis_index("tensor")
    g = s // GROUP
    m = s % GROUP
    base = g * GROUP
    chip = t // 2
    core = t % 2
    chips = tensor_count // 2
    groups = seq_count // GROUP
    rows, width = f_v.shape
    head = qg_ref.shape[1]
    toks = q_v.shape[0]
    heads = q_v.shape[1] // head
    scale = head ** (-0.5)
    has_next = g < groups - 1
    has_prev = g > 0
    inner = (chip % 3 + 1) // 2
    partner = (s, t + 1 - 2 * core)

    pending = []

    def finish():
        for wait in pending:
            wait()

    def when_done(condition, waits):
        def wait_all():
            @pl.when(condition)
            def _():
                for wait in waits:
                    wait()

        pending.append(wait_all)

    barrier = pltpu.get_barrier_semaphore()

    def greet(device):
        pl.semaphore_signal(barrier, inc=1, device_id=device, device_id_type=MESH)

    @pl.when(has_next)
    def _():
        greet((base + GROUP, t))
        greet((base + GROUP + 1, t))

    @pl.when(has_prev & (m < 2))
    def _():
        for e in range(GROUP):
            greet((base - GROUP + e, t))

    for off in range(1, GROUP):
        greet((base + (m + off) % GROUP, t))
    greet(partner)
    for off in range(1, chips):
        greet((s, ((chip + off) % chips) * 2 + core))

    step = width // W_CHUNKS
    loads = []
    for i in range(W_CHUNKS):
        part = pl.ds(i * step, step)
        loads.append([
            pltpu.make_async_copy(f_hbm.at[:, part], f_v.at[:, part], load_sem.at[3 * i]),
            pltpu.make_async_copy(wk_hbm.at[part, :], w_v.at[part, pl.ds(0, head)], load_sem.at[3 * i + 1]),
            pltpu.make_async_copy(wv_hbm.at[part, :], w_v.at[part, pl.ds(head, head)], load_sem.at[3 * i + 2]),
        ])
    q_load = pltpu.make_async_copy(q_hbm, q_v, load_sem.at[3 * W_CHUNKS])
    do_load = pltpu.make_async_copy(do_hbm, do_v, load_sem.at[3 * W_CHUNKS + 1])
    small_loads = [
        pltpu.make_async_copy(src, dst, small_sem.at[i])
        for i, (src, dst) in enumerate([
            (kg_hbm, kg_ref), (qg_hbm, qg_ref), (slot_hbm, slot_ref), (tiles_hbm, tiles_ref),
            (range_hbm, range_ref),
        ])
    ]
    small_loads[0].start()
    for group_loads in loads:
        for copy in group_loads:
            copy.start()
    q_load.start()
    do_load.start()
    for copy in small_loads[1:]:
        copy.start()

    acc = jnp.zeros((rows, 2 * head), F32)
    for i in range(W_CHUNKS):
        for copy in loads[i]:
            copy.wait()
        part = slice(i * step, (i + 1) * step)
        acc = acc + dot(f_v[:, part], w_v[part, :], ((1,), (0,)))
    small_loads[0].wait()
    raw = acc[:, :head]
    raw_v[...] = raw
    kinv = lax.rsqrt(jnp.mean(raw * raw, axis=-1, keepdims=True) + 1e-05)
    kv_in[m, :, :head] = (raw * kinv * kg_ref[...]).astype(BF16)
    kv_in[m, :, head:] = acc[:, head:].astype(BF16)

    peers = (
        GROUP - 1 + chips
        + jnp.where(has_next, 2, 0)
        + jnp.where(has_prev & (m < 2), GROUP, 0)
    )
    pl.semaphore_wait(barrier, peers)

    def remote(src, dst, send, recv, device):
        return pltpu.make_async_remote_copy(
            src_ref=src, dst_ref=dst, send_sem=send, recv_sem=recv,
            device_id=device, device_id_type=MESH,
        )

    def kv_cross():
        return remote(
            kv_in.at[m], kv_in.at[GROUP + m], kv_send.at[GROUP - 1], kv_recv.at[GROUP + m],
            (base + GROUP, t),
        )

    def kv_group(off):
        return remote(
            kv_in.at[m], kv_in.at[m], kv_send.at[off - 1], kv_recv.at[m],
            (base + (m + off) % GROUP, t),
        )

    def kv_arrived(slot):
        pltpu.make_async_copy(kv_in.at[slot], kv_in.at[slot], kv_recv.at[slot]).wait()

    @pl.when(has_next)
    def _():
        kv_cross().start()

    when_done(has_next, [lambda: kv_cross().wait_send()])

    for off in range(1, GROUP):
        kv_group(off).start()
        pending.append(lambda off=off: kv_group(off).wait_send())

    q_load.wait()
    for copy in small_loads[1:]:
        copy.wait()
    for h in range(heads):
        cols = slice(h * head, (h + 1) * head)
        x = q_v[:, cols].astype(F32)
        inv = lax.rsqrt(jnp.mean(x * x, axis=-1, keepdims=True) + 1e-05)
        inv_v[h] = jnp.broadcast_to(inv, (toks, head))
        normed = (x * inv * qg_ref[...]).astype(BF16)
        q16_v[:, cols] = normed
        qt_v[h] = normed.astype(F32).T.astype(BF16)

    blocks = range_ref.shape[1]
    per_block = toks // blocks
    block_of = lax.broadcasted_iota(jnp.int32, (1, toks), 1) // per_block
    row_of = lax.broadcasted_iota(jnp.int32, (rows, toks), 0)
    for j in range(LOOKBACK):
        image = s - (LOOKBACK - 1) + j
        live = tiles_ref[jnp.maximum(image, 0)] * TILE_ROWS
        limit = jnp.zeros((1, toks), jnp.int32)
        for b in range(blocks):
            seen = (range_ref[0, b] <= image) & (image < range_ref[1, b])
            limit = jnp.where(block_of == b, jnp.where(seen, live, 0), limit)
        bias_v[j * rows:(j + 1) * rows, :] = jnp.where(row_of < limit, 0.0, HIDDEN)
    do_load.wait()

    for off in range(1, GROUP):
        kv_arrived((m + off) % GROUP)
    ids = [slot_ref[base + e] for e in range(GROUP)]
    for j in range(LOOKBACK):
        image = s - (LOOKBACK - 1) + j
        chosen = jnp.zeros((rows, 2 * head), BF16)
        for e in range(GROUP):
            chosen = jnp.where(ids[e] == image, kv_in[e], chosen)
        kcat[j * rows:(j + 1) * rows, :] = chosen

    def kv_relay():
        return remote(
            kcat.at[pl.ds(rows, rows)], kv_in.at[GROUP], kv_send.at[GROUP], kv_recv.at[GROUP],
            (s + 1, t),
        )

    @pl.when(has_prev & (m == 0))
    def _():
        for e in range(GROUP):
            kv_arrived(GROUP + e)
        for j in reversed(range(LOOKBACK - 1)):
            image = s - (LOOKBACK - 1) + j
            chosen = kcat[j * rows:(j + 1) * rows, :]
            for e in range(GROUP):
                chosen = jnp.where(slot_ref[base - GROUP + e] == image, kv_in[GROUP + e], chosen)
            kcat[j * rows:(j + 1) * rows, :] = chosen
            if j == 1:
                kv_relay().start()

    when_done(has_prev & (m == 0), [lambda: kv_relay().wait_send()])

    @pl.when(has_prev & (m == 1))
    def _():
        kv_arrived(GROUP)
        kcat[:rows, :] = kv_in[GROUP]

    keys = kcat[:, :head]
    values = kcat[:, head:]
    for h in range(heads):
        cols = slice(h * head, (h + 1) * head)
        scores = dot(keys, qt_v[h], ((1,), (0,)))
        e = jnp.exp2(scores * (scale * LOG2E) + bias_v[...])
        total = jnp.sum(e, axis=0, keepdims=True)
        p = e * jnp.where(total > 0.0, 1.0 / total, 0.0)
        p_v[h] = p.astype(BF16)
        dp = dot(values, do_v[:, cols], ((1,), (1,)))
        delta = jnp.sum(p * dp, axis=0, keepdims=True)
        ds_v[h] = (p * (dp - delta)).astype(BF16)

    def image_grads(j):
        part = slice(j * rows, (j + 1) * rows)
        dk = jnp.zeros((rows, head), F32)
        dv = jnp.zeros((rows, head), F32)
        for h in range(heads):
            cols = slice(h * head, (h + 1) * head)
            dk = dk + dot(ds_v[h, part, :], q16_v[:, cols], ((1,), (0,)))
            dv = dv + dot(p_v[h, part, :], do_v[:, cols], ((1,), (0,)))
        g_v[j, :, :head] = dk * scale
        g_v[j, :, head:] = dv

    def for_slot(image_id, count):
        total = jnp.zeros((rows, 2 * head), F32)
        for j in range(count):
            total = jnp.where(image_id == s - (LOOKBACK - 1) + j, g_v[j], total)
        return total

    def cross_back(e):
        return remote(csend.at[e], crecv.at[m], c_send.at[e], c_recv.at[m], (base - GROUP + e, t))

    def send_cross_back(count):
        def send():
            grads = [g_v[j].astype(BF16) for j in range(count)]
            for e in range(GROUP):
                chosen = jnp.zeros((rows, 2 * head), BF16)
                for j in range(count):
                    image = s - (LOOKBACK - 1) + j
                    chosen = jnp.where(slot_ref[base - GROUP + e] == image, grads[j], chosen)
                csend[e] = chosen
                cross_back(e).start()

        return send

    image_grads(0)
    pl.when(has_prev & (m == 1))(send_cross_back(1))
    image_grads(1)
    pl.when(has_prev & (m == 0))(send_cross_back(2))
    when_done(has_prev & (m < 2), [lambda e=e: cross_back(e).wait_send() for e in range(GROUP)])
    image_grads(2)

    def group_back(off):
        return remote(
            gsend.at[off - 1], grecv.at[off - 1], g_send.at[off - 1], g_recv.at[off - 1],
            (base + (m + off) % GROUP, t),
        )

    for off in range(1, GROUP):
        gsend[off - 1] = for_slot(slot_ref[base + (m + off) % GROUP], LOOKBACK).astype(BF16)
        group_back(off).start()
        pending.append(lambda off=off: group_back(off).wait_send())

    for h in range(heads):
        cols = slice(h * head, (h + 1) * head)
        att_v[:, cols] = dot(p_v[h], values, ((0,), (0,))).astype(BF16)
        x = q_v[:, cols].astype(F32)
        inv = inv_v[h]
        up = dot(ds_v[h], keys, ((0,), (0,))) * (qg_ref[...] * scale)
        mean = jnp.mean(up * x, axis=-1, keepdims=True)
        gq_v[:, cols] = (inv * up - x * (inv * inv * inv) * mean).astype(BF16)
    att_store = pltpu.make_async_copy(att_v, att_hbm, store_sem.at[0])
    gq_store = pltpu.make_async_copy(gq_v, gq_hbm, store_sem.at[1])
    att_store.start()
    gq_store.start()
    pending.extend([att_store.wait, gq_store.wait])

    def arrived(buffer, sem, slot):
        pltpu.make_async_copy(buffer.at[slot], buffer.at[slot], sem.at[slot]).wait()
        return buffer[slot].astype(F32)

    g_v[0] = for_slot(slot_ref[s], LOOKBACK)
    for off in range(1, GROUP):
        group_back(off).wait_recv()
        g_v[0] = g_v[0] + grecv[off - 1].astype(F32)

    @pl.when(has_next)
    def _():
        for i in range(2):
            g_v[0] = g_v[0] + arrived(crecv, c_recv, i)

    raw = raw_v[...]
    kinv = lax.rsqrt(jnp.mean(raw * raw, axis=-1, keepdims=True) + 1e-05)
    up = g_v[0, :, :head] * kg_ref[...]
    mean = jnp.mean(up * raw, axis=-1, keepdims=True)
    a_v[:, :head] = (kinv * up - raw * (kinv * kinv * kinv) * mean).astype(BF16)
    a_v[:, head:] = g_v[0, :, head:].astype(BF16)

    out_cols = gf_v.shape[1]

    def term(owner):
        part = pl.ds(pl.multiple_of(owner * out_cols, out_cols), out_cols)
        return dot(a_v[...], w_v[part, :], ((1,), (1,)))

    def to_partner(i):
        return remote(psend.at[i], precv.at[i], p_send.at[i], p_recv.at[i], partner)

    mate = chip + (1 - 2 * (chip % 2))
    far_mate = chips - 1 - mate
    far_same = chips - 1 - chip
    order = [
        inner * far_same + (1 - inner) * far_same,
        inner * mate + (1 - inner) * far_mate,
        inner * far_mate + (1 - inner) * mate,
        chip,
    ]
    target = [inner * order[0] + (1 - inner) * mate, order[1], order[2]]
    landing = [3 - 2 * inner, 2 - 2 * inner, inner]

    def to_chip(i):
        return remote(
            bsend.at[i], brecv.at[landing[i]], b_send.at[i], b_recv.at[landing[i]],
            (s, target[i] * 2 + core),
        )

    def landed(slot):
        pltpu.make_async_copy(brecv.at[slot], brecv.at[slot], b_recv.at[slot]).wait()
        return brecv[slot].astype(F32)

    for i in range(chips):
        psend[i] = term(order[i] * 2 + 1 - core).astype(BF16)
        to_partner(i).start()
        pending.append(lambda i=i: to_partner(i).wait_send())
    for i in (0, 1, 3, 2):
        own = term(order[i] * 2 + core).astype(BF16).astype(F32)
        to_partner(i).wait_recv()
        both = own + precv[i].astype(F32)
        if i == 3:
            sum_v[...] = both
            continue
        bsend[i] = both.astype(BF16)
        if i == 2:
            @pl.when(inner == 1)
            def _():
                bsend[2] = (bsend[2].astype(F32) + landed(3)).astype(BF16)
        to_chip(i).start()
        pending.append(lambda i=i: to_chip(i).wait_send())
    sum_v[...] = sum_v[...] + landed(0)

    @pl.when(inner == 1)
    def _():
        sum_v[...] = sum_v[...] + landed(2)

    both = sum_v[...] + landed(1)
    gf_v[...] = both.astype(BF16)
    gf_store = pltpu.make_async_copy(gf_v, gf_hbm, store_sem.at[2])
    gf_store.start()
    pending.append(gf_store.wait)

    finish()


def local(
    queries, features, w_key, w_value, q_gain, k_gain, slot_image, image_tiles, image_range, d_out
):
    seq_count = lax.axis_size("seq")
    tensor_count = lax.axis_size("tensor")
    chips = tensor_count // 2
    toks, q_cols = queries.shape
    rows, width = features.shape
    head = q_gain.shape[0]
    heads = q_cols // head
    keys = LOOKBACK * rows
    out_cols = width // tensor_count
    dma = pltpu.SemaphoreType.DMA
    any_space = pl.BlockSpec(memory_space=pl.ANY)
    hbm = pl.BlockSpec(memory_space=pltpu.HBM)
    scratch = [
        pltpu.VMEM((1, head), F32),
        pltpu.VMEM((1, head), F32),
        pltpu.SMEM(slot_image.shape, jnp.int32),
        pltpu.SMEM(image_tiles.shape, jnp.int32),
        pltpu.SMEM(image_range.shape[::-1], jnp.int32),
        pltpu.VMEM((rows, width), BF16),
        pltpu.VMEM((width, 2 * head), BF16),
        pltpu.VMEM((toks, q_cols), BF16),
        pltpu.VMEM((toks, q_cols), BF16),
        pltpu.VMEM((toks, q_cols), BF16),
        pltpu.VMEM((toks, q_cols), BF16),
        pltpu.VMEM((rows, out_cols), BF16),
        pltpu.VMEM((rows, head), F32),
        pltpu.VMEM((2 * GROUP, rows, 2 * head), BF16),
        pltpu.VMEM((keys, 2 * head), BF16),
        pltpu.VMEM((toks, q_cols), BF16),
        pltpu.VMEM((heads, head, toks), BF16),
        pltpu.VMEM((heads, toks, head), F32),
        pltpu.VMEM((keys, toks), F32),
        pltpu.VMEM((heads, keys, toks), BF16),
        pltpu.VMEM((heads, keys, toks), BF16),
        pltpu.VMEM((LOOKBACK, rows, 2 * head), F32),
        pltpu.VMEM((GROUP - 1, rows, 2 * head), BF16),
        pltpu.VMEM((GROUP - 1, rows, 2 * head), BF16),
        pltpu.VMEM((GROUP, rows, 2 * head), BF16),
        pltpu.VMEM((2, rows, 2 * head), BF16),
        pltpu.VMEM((rows, 2 * head), BF16),
        pltpu.VMEM((chips, rows, out_cols), BF16),
        pltpu.VMEM((chips, rows, out_cols), BF16),
        pltpu.VMEM((chips - 1, rows, out_cols), BF16),
        pltpu.VMEM((chips, rows, out_cols), BF16),
        pltpu.VMEM((rows, out_cols), F32),
        dma((5,)),
        dma((3 * W_CHUNKS + 2,)),
        dma((3,)),
        dma((GROUP + 1,)),
        dma((2 * GROUP,)),
        dma((GROUP - 1,)),
        dma((GROUP - 1,)),
        dma((GROUP,)),
        dma((2,)),
        dma((chips,)),
        dma((chips,)),
        dma((chips - 1,)),
        dma((chips,)),
    ]
    return pl.pallas_call(
        functools.partial(kernel, seq_count, tensor_count),
        out_shape=(
            jax.ShapeDtypeStruct((toks, q_cols), BF16),
            jax.ShapeDtypeStruct((toks, q_cols), BF16),
            jax.ShapeDtypeStruct((rows, out_cols), BF16),
        ),
        in_specs=[hbm] * 10,
        out_specs=(any_space,) * 3,
        scratch_shapes=scratch,
        compiler_params=pltpu.CompilerParams(
            collective_id=0, has_side_effects=True, vmem_limit_bytes=105 * 512 * 1024
        ),
        cost_estimate=pl.CostEstimate(
            flops=1_300_000_000, bytes_accessed=5_500_000, transcendentals=600_000
        ),
    )(
        queries, features, w_key, w_value, q_gain.reshape(1, head), k_gain.reshape(1, head),
        slot_image, image_tiles, image_range.T, d_out,
    )


def solution(mesh):
    in_specs = (
        P("seq", "tensor"),
        P("seq", None),
        P(None, "tensor"),
        P(None, "tensor"),
        P(),
        P(),
        P(),
        P(),
        P("seq", None),
        P("seq", "tensor"),
    )
    out_specs = (P("seq", "tensor"), P("seq", "tensor"), P("seq", "tensor"))
    return jax.shard_map(local, mesh=mesh, in_specs=in_specs, out_specs=out_specs, check_vma=False)
```

```python
import functools

import jax
import jax.numpy as jnp
from jax import lax
from jax.experimental import pallas as pl
from jax.experimental.pallas import tpu as pltpu
from jax.sharding import PartitionSpec as P

TILE_ROWS = 24
GROUP = 4
LOOKBACK = 3
BF16 = jnp.bfloat16
F32 = jnp.float32
MESH = pl.DeviceIdType.MESH
LOG2E = 1.4426950408889634
HIDDEN = -1e30
W_CHUNKS = 4


def dot(a, b, contract):
    return lax.dot_general(a, b, (contract, ((), ())), preferred_element_type=F32)


def kernel(
    seq_count, tensor_count,
    q_hbm, f_hbm, wk_hbm, wv_hbm, qg_hbm, kg_hbm, slot_hbm, tiles_hbm, range_hbm, do_hbm,
    att_hbm, gq_hbm, gf_hbm,
    qg_ref, kg_ref, slot_ref, tiles_ref, range_ref,
    f_v, w_v, q_v, do_v, att_v, gq_v, gf_v,
    raw_v, kv_in, kcat, e_v, dp_v, total_v, weighted_v, q16_v, qt_v, inv_v, bias_v, p_v, ds_v,
    g_v, gsend, grecv, csend, crecv, a_v,
    psend, precv, bsend, brecv, sum_v,
    small_sem, load_sem, store_sem, kv_send, kv_recv, g_send, g_recv, c_send, c_recv,
    p_send, p_recv, b_send, b_recv,
):
    s = lax.axis_index("seq")
    t = lax.axis_index("tensor")
    g = s // GROUP
    m = s % GROUP
    base = g * GROUP
    chip = t // 2
    core = t % 2
    chips = tensor_count // 2
    groups = seq_count // GROUP
    rows, width = f_v.shape
    head = qg_ref.shape[1]
    toks = q_v.shape[0]
    heads = q_v.shape[1] // head
    scale = head ** (-0.5)
    has_next = g < groups - 1
    has_prev = g > 0
    inner = (chip % 3 + 1) // 2
    partner = (s, t + 1 - 2 * core)

    pending = []

    def finish():
        for wait in pending:
            wait()

    def when_done(condition, waits):
        def wait_all():
            @pl.when(condition)
            def _():
                for wait in waits:
                    wait()

        pending.append(wait_all)

    barrier = pltpu.get_barrier_semaphore()

    def greet(device):
        pl.semaphore_signal(barrier, inc=1, device_id=device, device_id_type=MESH)

    for off in range(1, GROUP):
        greet((base + (m + off) % GROUP, t))

    @pl.when(has_next)
    def _():
        greet((base + GROUP, t))
        greet((base + GROUP + 1, t))

    @pl.when(has_prev & (m < 2))
    def _():
        for e in range(GROUP):
            greet((base - GROUP + e, t))

    greet(partner)
    for off in range(1, chips):
        greet((s, ((chip + off) % chips) * 2 + core))

    step = width // W_CHUNKS
    loads = []
    for i in range(W_CHUNKS):
        part = pl.ds(i * step, step)
        loads.append([
            pltpu.make_async_copy(f_hbm.at[:, part], f_v.at[:, part], load_sem.at[3 * i]),
            pltpu.make_async_copy(wk_hbm.at[part, :], w_v.at[part, pl.ds(0, head)], load_sem.at[3 * i + 1]),
            pltpu.make_async_copy(wv_hbm.at[part, :], w_v.at[part, pl.ds(head, head)], load_sem.at[3 * i + 2]),
        ])
    q_load = pltpu.make_async_copy(q_hbm, q_v, load_sem.at[3 * W_CHUNKS])
    do_load = pltpu.make_async_copy(do_hbm, do_v, load_sem.at[3 * W_CHUNKS + 1])
    small_loads = [
        pltpu.make_async_copy(src, dst, small_sem.at[i])
        for i, (src, dst) in enumerate([
            (kg_hbm, kg_ref), (qg_hbm, qg_ref), (slot_hbm, slot_ref), (tiles_hbm, tiles_ref),
            (range_hbm, range_ref),
        ])
    ]
    small_loads[0].start()
    for group_loads in loads:
        for copy in group_loads:
            copy.start()
    for copy in small_loads[1:]:
        copy.start()

    acc = jnp.zeros((rows, 2 * head), F32)
    for i in range(W_CHUNKS):
        for copy in loads[i]:
            copy.wait()
        part = slice(i * step, (i + 1) * step)
        acc = acc + dot(f_v[:, part], w_v[part, :], ((1,), (0,)))
    q_load.start()
    do_load.start()
    small_loads[0].wait()
    raw = acc[:, :head]
    raw_v[...] = raw
    kinv = lax.rsqrt(jnp.mean(raw * raw, axis=-1, keepdims=True) + 1e-05)
    kv_in[m, :, :head] = (raw * kinv * kg_ref[...]).astype(BF16)
    kv_in[m, :, head:] = acc[:, head:].astype(BF16)

    peers = (
        GROUP - 1 + chips
        + jnp.where(has_next, 2, 0)
        + jnp.where(has_prev & (m < 2), GROUP, 0)
    )
    pl.semaphore_wait(barrier, peers)

    def remote(src, dst, send, recv, device):
        return pltpu.make_async_remote_copy(
            src_ref=src, dst_ref=dst, send_sem=send, recv_sem=recv,
            device_id=device, device_id_type=MESH,
        )

    def kv_cross():
        return remote(
            kv_in.at[m], kv_in.at[GROUP + m], kv_send.at[GROUP - 1], kv_recv.at[GROUP + m],
            (base + GROUP, t),
        )

    def kv_group(off):
        return remote(
            kv_in.at[m], kv_in.at[m], kv_send.at[off - 1], kv_recv.at[m],
            (base + (m + off) % GROUP, t),
        )

    def kv_arrived(slot):
        pltpu.make_async_copy(kv_in.at[slot], kv_in.at[slot], kv_recv.at[slot]).wait()

    @pl.when(has_next)
    def _():
        kv_cross().start()

    when_done(has_next, [lambda: kv_cross().wait_send()])

    for off in range(1, GROUP):
        kv_group(off).start()
        pending.append(lambda off=off: kv_group(off).wait_send())

    q_load.wait()
    for copy in small_loads[1:]:
        copy.wait()
    for h in range(heads):
        cols = slice(h * head, (h + 1) * head)
        x = q_v[:, cols].astype(F32)
        inv = lax.rsqrt(jnp.mean(x * x, axis=-1, keepdims=True) + 1e-05)
        inv_v[h] = jnp.broadcast_to(inv, (toks, head))
        normed = (x * inv * qg_ref[...]).astype(BF16)
        q16_v[:, cols] = normed
        qt_v[h] = normed.astype(F32).T.astype(BF16)

    blocks = range_ref.shape[1]
    per_block = toks // blocks
    block_of = lax.broadcasted_iota(jnp.int32, (1, toks), 1) // per_block
    row_of = lax.broadcasted_iota(jnp.int32, (rows, toks), 0)
    for j in range(LOOKBACK):
        image = s - (LOOKBACK - 1) + j
        live = tiles_ref[jnp.maximum(image, 0)] * TILE_ROWS
        limit = jnp.zeros((1, toks), jnp.int32)
        for b in range(blocks):
            seen = (range_ref[0, b] <= image) & (image < range_ref[1, b])
            limit = jnp.where(block_of == b, jnp.where(seen, live, 0), limit)
        bias_v[j * rows:(j + 1) * rows, :] = jnp.where(row_of < limit, 0.0, HIDDEN)
    do_load.wait()

    for off in range(1, GROUP):
        kv_arrived((m + off) % GROUP)
    ids = [slot_ref[base + e] for e in range(GROUP)]
    for j in range(LOOKBACK):
        image = s - (LOOKBACK - 1) + j
        chosen = jnp.zeros((rows, 2 * head), BF16)
        for e in range(GROUP):
            chosen = jnp.where(ids[e] == image, kv_in[e], chosen)
        kcat[j * rows:(j + 1) * rows, :] = chosen

    def scan(low, high, first):
        def some():
            part = slice(low * rows, high * rows)
            for h in range(heads):
                cols = slice(h * head, (h + 1) * head)
                scores = dot(kcat[part, :head], qt_v[h], ((1,), (0,)))
                e = jnp.exp2(scores * (scale * LOG2E) + bias_v[part, :])
                dp = dot(kcat[part, head:], do_v[:, cols], ((1,), (1,)))
                e_v[h, part, :] = e
                dp_v[h, part, :] = dp
                total = jnp.sum(e, axis=0, keepdims=True)
                weighted = jnp.sum(e * dp, axis=0, keepdims=True)
                total_v[h] = total if first else total_v[h] + total
                weighted_v[h] = weighted if first else weighted_v[h] + weighted

        return some

    def settle(j):
        part = slice(j * rows, (j + 1) * rows)
        for h in range(heads):
            total = total_v[h]
            inverse = jnp.where(total > 0.0, 1.0 / total, 0.0)
            p = e_v[h, part, :] * inverse
            p_v[h, part, :] = p.astype(BF16)
            ds_v[h, part, :] = (p * (dp_v[h, part, :] - weighted_v[h] * inverse)).astype(BF16)

    pl.when(m == 1)(scan(1, 3, True))

    def kv_relay():
        return remote(
            kcat.at[pl.ds(rows, rows)], kv_in.at[GROUP], kv_send.at[GROUP], kv_recv.at[GROUP],
            (s + 1, t),
        )

    @pl.when(has_prev & (m == 0))
    def _():
        for e in range(GROUP):
            kv_arrived(GROUP + e)
        for j in reversed(range(LOOKBACK - 1)):
            image = s - (LOOKBACK - 1) + j
            chosen = kcat[j * rows:(j + 1) * rows, :]
            for e in range(GROUP):
                chosen = jnp.where(slot_ref[base - GROUP + e] == image, kv_in[GROUP + e], chosen)
            kcat[j * rows:(j + 1) * rows, :] = chosen
            if j == 1:
                kv_relay().start()

    when_done(has_prev & (m == 0), [lambda: kv_relay().wait_send()])

    @pl.when(has_prev & (m == 1))
    def _():
        kv_arrived(GROUP)
        kcat[:rows, :] = kv_in[GROUP]

    pl.when(m == 1)(scan(0, 1, False))

    @pl.when(m != 1)
    def _():
        for h in range(heads):
            cols = slice(h * head, (h + 1) * head)
            scores = dot(kcat[:, :head], qt_v[h], ((1,), (0,)))
            e = jnp.exp2(scores * (scale * LOG2E) + bias_v[...])
            total = jnp.sum(e, axis=0, keepdims=True)
            p = e * jnp.where(total > 0.0, 1.0 / total, 0.0)
            p_v[h] = p.astype(BF16)
            dp = dot(kcat[:, head:], do_v[:, cols], ((1,), (1,)))
            delta = jnp.sum(p * dp, axis=0, keepdims=True)
            ds_v[h] = (p * (dp - delta)).astype(BF16)

    def image_grads(j):
        part = slice(j * rows, (j + 1) * rows)
        dk = jnp.zeros((rows, head), F32)
        dv = jnp.zeros((rows, head), F32)
        for h in range(heads):
            cols = slice(h * head, (h + 1) * head)
            dk = dk + dot(ds_v[h, part, :], q16_v[:, cols], ((1,), (0,)))
            dv = dv + dot(p_v[h, part, :], do_v[:, cols], ((1,), (0,)))
        g_v[j, :, :head] = dk * scale
        g_v[j, :, head:] = dv

    def for_slot(image_id, count):
        total = jnp.zeros((rows, 2 * head), F32)
        for j in range(count):
            total = jnp.where(image_id == s - (LOOKBACK - 1) + j, g_v[j], total)
        return total

    def cross_back(e):
        return remote(csend.at[e], crecv.at[m], c_send.at[e], c_recv.at[m], (base - GROUP + e, t))

    def send_cross_back(count):
        def send():
            grads = [g_v[j].astype(BF16) for j in range(count)]
            for e in range(GROUP):
                chosen = jnp.zeros((rows, 2 * head), BF16)
                for j in range(count):
                    image = s - (LOOKBACK - 1) + j
                    chosen = jnp.where(slot_ref[base - GROUP + e] == image, grads[j], chosen)
                csend[e] = chosen
                cross_back(e).start()

        return send

    pl.when(m == 1)(lambda: settle(0))
    image_grads(0)
    pl.when(has_prev & (m == 1))(send_cross_back(1))

    @pl.when(m == 1)
    def _():
        settle(1)
        settle(2)

    image_grads(1)
    pl.when(has_prev & (m == 0))(send_cross_back(2))
    when_done(has_prev & (m < 2), [lambda e=e: cross_back(e).wait_send() for e in range(GROUP)])
    image_grads(2)

    def group_back(off):
        return remote(
            gsend.at[off - 1], grecv.at[off - 1], g_send.at[off - 1], g_recv.at[off - 1],
            (base + (m + off) % GROUP, t),
        )

    for off in range(1, GROUP):
        gsend[off - 1] = for_slot(slot_ref[base + (m + off) % GROUP], LOOKBACK).astype(BF16)
        group_back(off).start()
        pending.append(lambda off=off: group_back(off).wait_send())

    keys = kcat[:, :head]
    values = kcat[:, head:]
    for h in range(heads):
        cols = slice(h * head, (h + 1) * head)
        att_v[:, cols] = dot(p_v[h], values, ((0,), (0,))).astype(BF16)
        x = q_v[:, cols].astype(F32)
        inv = inv_v[h]
        up = dot(ds_v[h], keys, ((0,), (0,))) * (qg_ref[...] * scale)
        mean = jnp.mean(up * x, axis=-1, keepdims=True)
        gq_v[:, cols] = (inv * up - x * (inv * inv * inv) * mean).astype(BF16)
    att_store = pltpu.make_async_copy(att_v, att_hbm, store_sem.at[0])
    gq_store = pltpu.make_async_copy(gq_v, gq_hbm, store_sem.at[1])
    att_store.start()
    gq_store.start()
    pending.extend([att_store.wait, gq_store.wait])

    def arrived(buffer, sem, slot):
        pltpu.make_async_copy(buffer.at[slot], buffer.at[slot], sem.at[slot]).wait()
        return buffer[slot].astype(F32)

    g_v[0] = for_slot(slot_ref[s], LOOKBACK)
    for off in range(1, GROUP):
        group_back(off).wait_recv()
        g_v[0] = g_v[0] + grecv[off - 1].astype(F32)

    @pl.when(has_next)
    def _():
        for i in range(2):
            g_v[0] = g_v[0] + arrived(crecv, c_recv, i)

    raw = raw_v[...]
    kinv = lax.rsqrt(jnp.mean(raw * raw, axis=-1, keepdims=True) + 1e-05)
    up = g_v[0, :, :head] * kg_ref[...]
    mean = jnp.mean(up * raw, axis=-1, keepdims=True)
    a_v[:, :head] = (kinv * up - raw * (kinv * kinv * kinv) * mean).astype(BF16)
    a_v[:, head:] = g_v[0, :, head:].astype(BF16)

    out_cols = gf_v.shape[1]

    def term(owner):
        part = pl.ds(pl.multiple_of(owner * out_cols, out_cols), out_cols)
        return dot(a_v[...], w_v[part, :], ((1,), (1,)))

    def to_partner(i):
        return remote(psend.at[i], precv.at[i], p_send.at[i], p_recv.at[i], partner)

    mate = chip + (1 - 2 * (chip % 2))
    far_mate = chips - 1 - mate
    far_same = chips - 1 - chip
    order = [
        inner * far_same + (1 - inner) * far_same,
        inner * mate + (1 - inner) * far_mate,
        inner * far_mate + (1 - inner) * mate,
        chip,
    ]
    target = [inner * order[0] + (1 - inner) * mate, order[1], order[2]]
    landing = [3 - 2 * inner, 2 - 2 * inner, inner]

    def to_chip(i):
        return remote(
            bsend.at[i], brecv.at[landing[i]], b_send.at[i], b_recv.at[landing[i]],
            (s, target[i] * 2 + core),
        )

    def landed(slot):
        pltpu.make_async_copy(brecv.at[slot], brecv.at[slot], b_recv.at[slot]).wait()
        return brecv[slot].astype(F32)

    for i in range(chips):
        psend[i] = term(order[i] * 2 + 1 - core).astype(BF16)
        to_partner(i).start()
        pending.append(lambda i=i: to_partner(i).wait_send())
    for i in (0, 1, 3, 2):
        own = term(order[i] * 2 + core).astype(BF16).astype(F32)
        to_partner(i).wait_recv()
        both = own + precv[i].astype(F32)
        if i == 3:
            sum_v[...] = both
            continue
        bsend[i] = both.astype(BF16)
        if i == 2:
            @pl.when(inner == 1)
            def _():
                bsend[2] = (bsend[2].astype(F32) + landed(3)).astype(BF16)
        to_chip(i).start()
        pending.append(lambda i=i: to_chip(i).wait_send())
    sum_v[...] = sum_v[...] + landed(0)

    @pl.when(inner == 1)
    def _():
        sum_v[...] = sum_v[...] + landed(2)

    both = sum_v[...] + landed(1)
    gf_v[...] = both.astype(BF16)
    gf_store = pltpu.make_async_copy(gf_v, gf_hbm, store_sem.at[2])
    gf_store.start()
    pending.append(gf_store.wait)

    finish()


def local(
    queries, features, w_key, w_value, q_gain, k_gain, slot_image, image_tiles, image_range, d_out
):
    seq_count = lax.axis_size("seq")
    tensor_count = lax.axis_size("tensor")
    chips = tensor_count // 2
    toks, q_cols = queries.shape
    rows, width = features.shape
    head = q_gain.shape[0]
    heads = q_cols // head
    keys = LOOKBACK * rows
    out_cols = width // tensor_count
    dma = pltpu.SemaphoreType.DMA
    any_space = pl.BlockSpec(memory_space=pl.ANY)
    hbm = pl.BlockSpec(memory_space=pltpu.HBM)
    scratch = [
        pltpu.VMEM((1, head), F32),
        pltpu.VMEM((1, head), F32),
        pltpu.SMEM(slot_image.shape, jnp.int32),
        pltpu.SMEM(image_tiles.shape, jnp.int32),
        pltpu.SMEM(image_range.shape[::-1], jnp.int32),
        pltpu.VMEM((rows, width), BF16),
        pltpu.VMEM((width, 2 * head), BF16),
        pltpu.VMEM((toks, q_cols), BF16),
        pltpu.VMEM((toks, q_cols), BF16),
        pltpu.VMEM((toks, q_cols), BF16),
        pltpu.VMEM((toks, q_cols), BF16),
        pltpu.VMEM((rows, out_cols), BF16),
        pltpu.VMEM((rows, head), F32),
        pltpu.VMEM((2 * GROUP, rows, 2 * head), BF16),
        pltpu.VMEM((keys, 2 * head), BF16),
        pltpu.VMEM((heads, keys, toks), F32),
        pltpu.VMEM((heads, keys, toks), F32),
        pltpu.VMEM((heads, 1, toks), F32),
        pltpu.VMEM((heads, 1, toks), F32),
        pltpu.VMEM((toks, q_cols), BF16),
        pltpu.VMEM((heads, head, toks), BF16),
        pltpu.VMEM((heads, toks, head), F32),
        pltpu.VMEM((keys, toks), F32),
        pltpu.VMEM((heads, keys, toks), BF16),
        pltpu.VMEM((heads, keys, toks), BF16),
        pltpu.VMEM((LOOKBACK, rows, 2 * head), F32),
        pltpu.VMEM((GROUP - 1, rows, 2 * head), BF16),
        pltpu.VMEM((GROUP - 1, rows, 2 * head), BF16),
        pltpu.VMEM((GROUP, rows, 2 * head), BF16),
        pltpu.VMEM((2, rows, 2 * head), BF16),
        pltpu.VMEM((rows, 2 * head), BF16),
        pltpu.VMEM((chips, rows, out_cols), BF16),
        pltpu.VMEM((chips, rows, out_cols), BF16),
        pltpu.VMEM((chips - 1, rows, out_cols), BF16),
        pltpu.VMEM((chips, rows, out_cols), BF16),
        pltpu.VMEM((rows, out_cols), F32),
        dma((5,)),
        dma((3 * W_CHUNKS + 2,)),
        dma((3,)),
        dma((GROUP + 1,)),
        dma((2 * GROUP,)),
        dma((GROUP - 1,)),
        dma((GROUP - 1,)),
        dma((GROUP,)),
        dma((2,)),
        dma((chips,)),
        dma((chips,)),
        dma((chips - 1,)),
        dma((chips,)),
    ]
    return pl.pallas_call(
        functools.partial(kernel, seq_count, tensor_count),
        out_shape=(
            jax.ShapeDtypeStruct((toks, q_cols), BF16),
            jax.ShapeDtypeStruct((toks, q_cols), BF16),
            jax.ShapeDtypeStruct((rows, out_cols), BF16),
        ),
        in_specs=[hbm] * 10,
        out_specs=(any_space,) * 3,
        scratch_shapes=scratch,
        compiler_params=pltpu.CompilerParams(
            collective_id=0, has_side_effects=True, vmem_limit_bytes=105 * 512 * 1024
        ),
        cost_estimate=pl.CostEstimate(
            flops=1_300_000_000, bytes_accessed=5_500_000, transcendentals=600_000
        ),
    )(
        queries, features, w_key, w_value, q_gain.reshape(1, head), k_gain.reshape(1, head),
        slot_image, image_tiles, image_range.T, d_out,
    )


def solution(mesh):
    in_specs = (
        P("seq", "tensor"),
        P("seq", None),
        P(None, "tensor"),
        P(None, "tensor"),
        P(),
        P(),
        P(),
        P(),
        P("seq", None),
        P("seq", "tensor"),
    )
    out_specs = (P("seq", "tensor"), P("seq", "tensor"), P("seq", "tensor"))
    return jax.shard_map(local, mesh=mesh, in_specs=in_specs, out_specs=out_specs, check_vma=False)
```

```python
import functools

import jax
import jax.numpy as jnp
from jax import lax
from jax.experimental import pallas as pl
from jax.experimental.pallas import tpu as pltpu
from jax.sharding import PartitionSpec as P

TILE_ROWS = 24
GROUP = 4
LOOKBACK = 3
BF16 = jnp.bfloat16
F32 = jnp.float32
MESH = pl.DeviceIdType.MESH
LOG2E = 1.4426950408889634
HIDDEN = -1e30
W_CHUNKS = 4


def dot(a, b, contract):
    return lax.dot_general(a, b, (contract, ((), ())), preferred_element_type=F32)


def kernel(
    seq_count, tensor_count,
    q_hbm, f_hbm, wk_hbm, wv_hbm, qg_hbm, kg_hbm, slot_hbm, tiles_hbm, range_hbm, do_hbm,
    att_hbm, gq_hbm, gf_hbm,
    qg_ref, kg_ref, slot_ref, tiles_ref, range_ref,
    f_v, w_v, q_v, do_v, att_v, gq_v, gf_v,
    raw_v, kv_in, kcat, e_v, dp_v, total_v, weighted_v, q16_v, qt_v, inv_v, bias_v, p_v, ds_v,
    g_v, gsend, grecv, csend, crecv, a_v,
    psend, precv, bsend, brecv, sum_v,
    small_sem, load_sem, store_sem, kv_send, kv_recv, g_send, g_recv, c_send, c_recv,
    p_send, p_recv, b_send, b_recv,
):
    s = lax.axis_index("seq")
    t = lax.axis_index("tensor")
    g = s // GROUP
    m = s % GROUP
    base = g * GROUP
    chip = t // 2
    core = t % 2
    chips = tensor_count // 2
    groups = seq_count // GROUP
    rows, width = f_v.shape
    head = qg_ref.shape[1]
    toks = q_v.shape[0]
    heads = q_v.shape[1] // head
    scale = head ** (-0.5)
    has_next = g < groups - 1
    has_prev = g > 0
    inner = (chip % 3 + 1) // 2
    partner = (s, t + 1 - 2 * core)

    pending = []

    def finish():
        for wait in pending:
            wait()

    def when_done(condition, waits):
        def wait_all():
            @pl.when(condition)
            def _():
                for wait in waits:
                    wait()

        pending.append(wait_all)

    barrier = pltpu.get_barrier_semaphore()

    def greet(device):
        pl.semaphore_signal(barrier, inc=1, device_id=device, device_id_type=MESH)

    for off in range(1, GROUP):
        greet((base + (m + off) % GROUP, t))

    @pl.when(has_next)
    def _():
        greet((base + GROUP, t))
        greet((base + GROUP + 1, t))

    @pl.when(has_prev & (m < 2))
    def _():
        for e in range(GROUP):
            greet((base - GROUP + e, t))

    greet(partner)
    for off in range(1, chips):
        greet((s, ((chip + off) % chips) * 2 + core))

    step = width // W_CHUNKS
    loads = []
    for i in range(W_CHUNKS):
        part = pl.ds(i * step, step)
        loads.append([
            pltpu.make_async_copy(f_hbm.at[:, part], f_v.at[:, part], load_sem.at[3 * i]),
            pltpu.make_async_copy(wk_hbm.at[part, :], w_v.at[part, pl.ds(0, head)], load_sem.at[3 * i + 1]),
            pltpu.make_async_copy(wv_hbm.at[part, :], w_v.at[part, pl.ds(head, head)], load_sem.at[3 * i + 2]),
        ])
    q_load = pltpu.make_async_copy(q_hbm, q_v, load_sem.at[3 * W_CHUNKS])
    do_load = pltpu.make_async_copy(do_hbm, do_v, load_sem.at[3 * W_CHUNKS + 1])
    small_loads = [
        pltpu.make_async_copy(src, dst, small_sem.at[i])
        for i, (src, dst) in enumerate([
            (kg_hbm, kg_ref), (qg_hbm, qg_ref), (slot_hbm, slot_ref), (tiles_hbm, tiles_ref),
            (range_hbm, range_ref),
        ])
    ]
    small_loads[0].start()
    for group_loads in loads:
        for copy in group_loads:
            copy.start()
    for copy in small_loads[1:]:
        copy.start()

    acc = jnp.zeros((rows, 2 * head), F32)
    for i in range(W_CHUNKS):
        for copy in loads[i]:
            copy.wait()
        part = slice(i * step, (i + 1) * step)
        acc = acc + dot(f_v[:, part], w_v[part, :], ((1,), (0,)))
    q_load.start()
    do_load.start()
    small_loads[0].wait()
    raw = acc[:, :head]
    raw_v[...] = raw
    kinv = lax.rsqrt(jnp.mean(raw * raw, axis=-1, keepdims=True) + 1e-05)
    kv_in[m, :, :head] = (raw * kinv * kg_ref[...]).astype(BF16)
    kv_in[m, :, head:] = acc[:, head:].astype(BF16)

    peers = (
        GROUP - 1 + chips
        + jnp.where(has_next, 2, 0)
        + jnp.where(has_prev & (m < 2), GROUP, 0)
    )
    pl.semaphore_wait(barrier, peers)

    def remote(src, dst, send, recv, device):
        return pltpu.make_async_remote_copy(
            src_ref=src, dst_ref=dst, send_sem=send, recv_sem=recv,
            device_id=device, device_id_type=MESH,
        )

    near_next = has_next & (g % 2 == 0)
    near_prev = has_prev & (g % 2 == 1)
    far_prev = has_prev & (g % 2 == 0)

    def kv_cross(i):
        return remote(
            kv_in.at[m], kv_in.at[GROUP + m], kv_send.at[GROUP - 1 + 2 * i], kv_recv.at[GROUP + m],
            (base + GROUP + i, t),
        )

    def kv_group(off):
        return remote(
            kv_in.at[m], kv_in.at[m], kv_send.at[off - 1], kv_recv.at[m],
            (base + (m + off) % GROUP, t),
        )

    def kv_arrived(slot):
        pltpu.make_async_copy(kv_in.at[slot], kv_in.at[slot], kv_recv.at[slot]).wait()

    @pl.when(has_next)
    def _():
        kv_cross(0).start()

    @pl.when(near_next)
    def _():
        kv_cross(1).start()

    when_done(has_next, [lambda: kv_cross(0).wait_send()])
    when_done(near_next, [lambda: kv_cross(1).wait_send()])

    for off in range(1, GROUP):
        kv_group(off).start()
        pending.append(lambda off=off: kv_group(off).wait_send())

    q_load.wait()
    for copy in small_loads[1:]:
        copy.wait()
    for h in range(heads):
        cols = slice(h * head, (h + 1) * head)
        x = q_v[:, cols].astype(F32)
        inv = lax.rsqrt(jnp.mean(x * x, axis=-1, keepdims=True) + 1e-05)
        inv_v[h] = jnp.broadcast_to(inv, (toks, head))
        normed = (x * inv * qg_ref[...]).astype(BF16)
        q16_v[:, cols] = normed
        qt_v[h] = normed.astype(F32).T.astype(BF16)

    blocks = range_ref.shape[1]
    per_block = toks // blocks
    block_of = lax.broadcasted_iota(jnp.int32, (1, toks), 1) // per_block
    row_of = lax.broadcasted_iota(jnp.int32, (rows, toks), 0)
    for j in range(LOOKBACK):
        image = s - (LOOKBACK - 1) + j
        live = tiles_ref[jnp.maximum(image, 0)] * TILE_ROWS
        limit = jnp.zeros((1, toks), jnp.int32)
        for b in range(blocks):
            seen = (range_ref[0, b] <= image) & (image < range_ref[1, b])
            limit = jnp.where(block_of == b, jnp.where(seen, live, 0), limit)
        bias_v[j * rows:(j + 1) * rows, :] = jnp.where(row_of < limit, 0.0, HIDDEN)
    do_load.wait()

    for off in range(1, GROUP):
        kv_arrived((m + off) % GROUP)
    ids = [slot_ref[base + e] for e in range(GROUP)]
    for j in range(LOOKBACK):
        image = s - (LOOKBACK - 1) + j
        chosen = jnp.zeros((rows, 2 * head), BF16)
        for e in range(GROUP):
            chosen = jnp.where(ids[e] == image, kv_in[e], chosen)
        kcat[j * rows:(j + 1) * rows, :] = chosen

    def scan(low, high, first):
        def some():
            part = slice(low * rows, high * rows)
            for h in range(heads):
                cols = slice(h * head, (h + 1) * head)
                scores = dot(kcat[part, :head], qt_v[h], ((1,), (0,)))
                e = jnp.exp2(scores * (scale * LOG2E) + bias_v[part, :])
                dp = dot(kcat[part, head:], do_v[:, cols], ((1,), (1,)))
                e_v[h, part, :] = e
                dp_v[h, part, :] = dp
                total = jnp.sum(e, axis=0, keepdims=True)
                weighted = jnp.sum(e * dp, axis=0, keepdims=True)
                total_v[h] = total if first else total_v[h] + total
                weighted_v[h] = weighted if first else weighted_v[h] + weighted

        return some

    def settle(j):
        part = slice(j * rows, (j + 1) * rows)
        for h in range(heads):
            total = total_v[h]
            inverse = jnp.where(total > 0.0, 1.0 / total, 0.0)
            p = e_v[h, part, :] * inverse
            p_v[h, part, :] = p.astype(BF16)
            ds_v[h, part, :] = (p * (dp_v[h, part, :] - weighted_v[h] * inverse)).astype(BF16)

    pl.when(m == 1)(scan(1, 3, True))

    def kv_relay():
        return remote(
            kcat.at[pl.ds(rows, rows)], kv_in.at[GROUP], kv_send.at[GROUP], kv_recv.at[GROUP],
            (s + 1, t),
        )

    @pl.when(has_prev & (m == 0))
    def _():
        for e in range(GROUP):
            kv_arrived(GROUP + e)
        for j in reversed(range(LOOKBACK - 1)):
            image = s - (LOOKBACK - 1) + j
            chosen = kcat[j * rows:(j + 1) * rows, :]
            for e in range(GROUP):
                chosen = jnp.where(slot_ref[base - GROUP + e] == image, kv_in[GROUP + e], chosen)
            kcat[j * rows:(j + 1) * rows, :] = chosen
            if j == 1:
                pl.when(far_prev)(lambda: kv_relay().start())

    when_done(far_prev & (m == 0), [lambda: kv_relay().wait_send()])

    @pl.when(far_prev & (m == 1))
    def _():
        kv_arrived(GROUP)
        kcat[:rows, :] = kv_in[GROUP]

    @pl.when(near_prev & (m == 1))
    def _():
        for e in range(GROUP):
            kv_arrived(GROUP + e)
        chosen = jnp.zeros((rows, 2 * head), BF16)
        for e in range(GROUP):
            held = slot_ref[base - GROUP + e] == s - (LOOKBACK - 1)
            chosen = jnp.where(held, kv_in[GROUP + e], chosen)
        kcat[:rows, :] = chosen

    pl.when(m == 1)(scan(0, 1, False))

    @pl.when(m != 1)
    def _():
        for h in range(heads):
            cols = slice(h * head, (h + 1) * head)
            scores = dot(kcat[:, :head], qt_v[h], ((1,), (0,)))
            e = jnp.exp2(scores * (scale * LOG2E) + bias_v[...])
            total = jnp.sum(e, axis=0, keepdims=True)
            p = e * jnp.where(total > 0.0, 1.0 / total, 0.0)
            p_v[h] = p.astype(BF16)
            dp = dot(kcat[:, head:], do_v[:, cols], ((1,), (1,)))
            delta = jnp.sum(p * dp, axis=0, keepdims=True)
            ds_v[h] = (p * (dp - delta)).astype(BF16)

    def image_grads(j):
        part = slice(j * rows, (j + 1) * rows)
        dk = jnp.zeros((rows, head), F32)
        dv = jnp.zeros((rows, head), F32)
        for h in range(heads):
            cols = slice(h * head, (h + 1) * head)
            dk = dk + dot(ds_v[h, part, :], q16_v[:, cols], ((1,), (0,)))
            dv = dv + dot(p_v[h, part, :], do_v[:, cols], ((1,), (0,)))
        g_v[j, :, :head] = dk * scale
        g_v[j, :, head:] = dv

    def for_slot(image_id, count):
        total = jnp.zeros((rows, 2 * head), F32)
        for j in range(count):
            total = jnp.where(image_id == s - (LOOKBACK - 1) + j, g_v[j], total)
        return total

    def cross_back(e):
        return remote(csend.at[e], crecv.at[m], c_send.at[e], c_recv.at[m], (base - GROUP + e, t))

    def send_cross_back(count):
        def send():
            grads = [g_v[j].astype(BF16) for j in range(count)]
            for e in range(GROUP):
                chosen = jnp.zeros((rows, 2 * head), BF16)
                for j in range(count):
                    image = s - (LOOKBACK - 1) + j
                    chosen = jnp.where(slot_ref[base - GROUP + e] == image, grads[j], chosen)
                csend[e] = chosen
                cross_back(e).start()

        return send

    pl.when(m == 1)(lambda: settle(0))
    image_grads(0)
    pl.when(has_prev & (m == 1))(send_cross_back(1))

    @pl.when(m == 1)
    def _():
        settle(1)
        settle(2)

    image_grads(1)
    pl.when(has_prev & (m == 0))(send_cross_back(2))
    when_done(has_prev & (m < 2), [lambda e=e: cross_back(e).wait_send() for e in range(GROUP)])
    image_grads(2)

    def group_back(off):
        return remote(
            gsend.at[off - 1], grecv.at[off - 1], g_send.at[off - 1], g_recv.at[off - 1],
            (base + (m + off) % GROUP, t),
        )

    for off in range(1, GROUP):
        gsend[off - 1] = for_slot(slot_ref[base + (m + off) % GROUP], LOOKBACK).astype(BF16)
        group_back(off).start()
        pending.append(lambda off=off: group_back(off).wait_send())

    keys = kcat[:, :head]
    values = kcat[:, head:]
    for h in range(heads):
        cols = slice(h * head, (h + 1) * head)
        att_v[:, cols] = dot(p_v[h], values, ((0,), (0,))).astype(BF16)
        x = q_v[:, cols].astype(F32)
        inv = inv_v[h]
        up = dot(ds_v[h], keys, ((0,), (0,))) * (qg_ref[...] * scale)
        mean = jnp.mean(up * x, axis=-1, keepdims=True)
        gq_v[:, cols] = (inv * up - x * (inv * inv * inv) * mean).astype(BF16)
    att_store = pltpu.make_async_copy(att_v, att_hbm, store_sem.at[0])
    gq_store = pltpu.make_async_copy(gq_v, gq_hbm, store_sem.at[1])
    att_store.start()
    gq_store.start()
    pending.extend([att_store.wait, gq_store.wait])

    def arrived(buffer, sem, slot):
        pltpu.make_async_copy(buffer.at[slot], buffer.at[slot], sem.at[slot]).wait()
        return buffer[slot].astype(F32)

    g_v[0] = for_slot(slot_ref[s], LOOKBACK)
    for off in range(1, GROUP):
        group_back(off).wait_recv()
        g_v[0] = g_v[0] + grecv[off - 1].astype(F32)

    @pl.when(has_next)
    def _():
        for i in range(2):
            g_v[0] = g_v[0] + arrived(crecv, c_recv, i)

    raw = raw_v[...]
    kinv = lax.rsqrt(jnp.mean(raw * raw, axis=-1, keepdims=True) + 1e-05)
    up = g_v[0, :, :head] * kg_ref[...]
    mean = jnp.mean(up * raw, axis=-1, keepdims=True)
    a_v[:, :head] = (kinv * up - raw * (kinv * kinv * kinv) * mean).astype(BF16)
    a_v[:, head:] = g_v[0, :, head:].astype(BF16)

    out_cols = gf_v.shape[1]

    def term(owner):
        part = pl.ds(pl.multiple_of(owner * out_cols, out_cols), out_cols)
        return dot(a_v[...], w_v[part, :], ((1,), (1,)))

    def to_partner(i):
        return remote(psend.at[i], precv.at[i], p_send.at[i], p_recv.at[i], partner)

    mate = chip + (1 - 2 * (chip % 2))
    far_mate = chips - 1 - mate
    far_same = chips - 1 - chip
    order = [
        inner * far_same + (1 - inner) * far_same,
        inner * mate + (1 - inner) * far_mate,
        inner * far_mate + (1 - inner) * mate,
        chip,
    ]
    target = [inner * order[0] + (1 - inner) * mate, order[1], order[2]]
    landing = [3 - 2 * inner, 2 - 2 * inner, inner]

    def to_chip(i):
        return remote(
            bsend.at[i], brecv.at[landing[i]], b_send.at[i], b_recv.at[landing[i]],
            (s, target[i] * 2 + core),
        )

    def landed(slot):
        pltpu.make_async_copy(brecv.at[slot], brecv.at[slot], b_recv.at[slot]).wait()
        return brecv[slot].astype(F32)

    for i in range(chips):
        psend[i] = term(order[i] * 2 + 1 - core).astype(BF16)
        to_partner(i).start()
        pending.append(lambda i=i: to_partner(i).wait_send())
    for i in (0, 1, 3, 2):
        own = term(order[i] * 2 + core).astype(BF16).astype(F32)
        to_partner(i).wait_recv()
        both = own + precv[i].astype(F32)
        if i == 3:
            sum_v[...] = both
            continue
        bsend[i] = both.astype(BF16)
        if i == 2:
            @pl.when(inner == 1)
            def _():
                bsend[2] = (bsend[2].astype(F32) + landed(3)).astype(BF16)
        to_chip(i).start()
        pending.append(lambda i=i: to_chip(i).wait_send())
    sum_v[...] = sum_v[...] + landed(0)

    @pl.when(inner == 1)
    def _():
        sum_v[...] = sum_v[...] + landed(2)

    both = sum_v[...] + landed(1)
    gf_v[...] = both.astype(BF16)
    gf_store = pltpu.make_async_copy(gf_v, gf_hbm, store_sem.at[2])
    gf_store.start()
    pending.append(gf_store.wait)

    finish()


def local(
    queries, features, w_key, w_value, q_gain, k_gain, slot_image, image_tiles, image_range, d_out
):
    seq_count = lax.axis_size("seq")
    tensor_count = lax.axis_size("tensor")
    chips = tensor_count // 2
    toks, q_cols = queries.shape
    rows, width = features.shape
    head = q_gain.shape[0]
    heads = q_cols // head
    keys = LOOKBACK * rows
    out_cols = width // tensor_count
    dma = pltpu.SemaphoreType.DMA
    any_space = pl.BlockSpec(memory_space=pl.ANY)
    hbm = pl.BlockSpec(memory_space=pltpu.HBM)
    scratch = [
        pltpu.VMEM((1, head), F32),
        pltpu.VMEM((1, head), F32),
        pltpu.SMEM(slot_image.shape, jnp.int32),
        pltpu.SMEM(image_tiles.shape, jnp.int32),
        pltpu.SMEM(image_range.shape[::-1], jnp.int32),
        pltpu.VMEM((rows, width), BF16),
        pltpu.VMEM((width, 2 * head), BF16),
        pltpu.VMEM((toks, q_cols), BF16),
        pltpu.VMEM((toks, q_cols), BF16),
        pltpu.VMEM((toks, q_cols), BF16),
        pltpu.VMEM((toks, q_cols), BF16),
        pltpu.VMEM((rows, out_cols), BF16),
        pltpu.VMEM((rows, head), F32),
        pltpu.VMEM((2 * GROUP, rows, 2 * head), BF16),
        pltpu.VMEM((keys, 2 * head), BF16),
        pltpu.VMEM((heads, keys, toks), F32),
        pltpu.VMEM((heads, keys, toks), F32),
        pltpu.VMEM((heads, 1, toks), F32),
        pltpu.VMEM((heads, 1, toks), F32),
        pltpu.VMEM((toks, q_cols), BF16),
        pltpu.VMEM((heads, head, toks), BF16),
        pltpu.VMEM((heads, toks, head), F32),
        pltpu.VMEM((keys, toks), F32),
        pltpu.VMEM((heads, keys, toks), BF16),
        pltpu.VMEM((heads, keys, toks), BF16),
        pltpu.VMEM((LOOKBACK, rows, 2 * head), F32),
        pltpu.VMEM((GROUP - 1, rows, 2 * head), BF16),
        pltpu.VMEM((GROUP - 1, rows, 2 * head), BF16),
        pltpu.VMEM((GROUP, rows, 2 * head), BF16),
        pltpu.VMEM((2, rows, 2 * head), BF16),
        pltpu.VMEM((rows, 2 * head), BF16),
        pltpu.VMEM((chips, rows, out_cols), BF16),
        pltpu.VMEM((chips, rows, out_cols), BF16),
        pltpu.VMEM((chips - 1, rows, out_cols), BF16),
        pltpu.VMEM((chips, rows, out_cols), BF16),
        pltpu.VMEM((rows, out_cols), F32),
        dma((5,)),
        dma((3 * W_CHUNKS + 2,)),
        dma((3,)),
        dma((GROUP + 2,)),
        dma((2 * GROUP,)),
        dma((GROUP - 1,)),
        dma((GROUP - 1,)),
        dma((GROUP,)),
        dma((2,)),
        dma((chips,)),
        dma((chips,)),
        dma((chips - 1,)),
        dma((chips,)),
    ]
    return pl.pallas_call(
        functools.partial(kernel, seq_count, tensor_count),
        out_shape=(
            jax.ShapeDtypeStruct((toks, q_cols), BF16),
            jax.ShapeDtypeStruct((toks, q_cols), BF16),
            jax.ShapeDtypeStruct((rows, out_cols), BF16),
        ),
        in_specs=[hbm] * 10,
        out_specs=(any_space,) * 3,
        scratch_shapes=scratch,
        compiler_params=pltpu.CompilerParams(
            collective_id=0, has_side_effects=True, vmem_limit_bytes=105 * 512 * 1024
        ),
        cost_estimate=pl.CostEstimate(
            flops=1_300_000_000, bytes_accessed=5_500_000, transcendentals=600_000
        ),
    )(
        queries, features, w_key, w_value, q_gain.reshape(1, head), k_gain.reshape(1, head),
        slot_image, image_tiles, image_range.T, d_out,
    )


def solution(mesh):
    in_specs = (
        P("seq", "tensor"),
        P("seq", None),
        P(None, "tensor"),
        P(None, "tensor"),
        P(),
        P(),
        P(),
        P(),
        P("seq", None),
        P("seq", "tensor"),
    )
    out_specs = (P("seq", "tensor"), P("seq", "tensor"), P("seq", "tensor"))
    return jax.shard_map(local, mesh=mesh, in_specs=in_specs, out_specs=out_specs, check_vma=False)
```
